256 devices in a mesh: tm: 32 (over x, y, core), heads: 8 (over z).
Axes of the slice: x: 4, y: 4, z: 8, core: 2. Of those that a mesh axis runs over, the one named last changes fastest.
Arguments:
- query_raw: bfloat16 [4096, 6144], P('tm', 'heads'), may hold values from -80 to 80
- key_raw: bfloat16 [4096, 6144], P('tm', 'heads'), may hold values from -80 to 80
- values: bfloat16 [4096, 6144], P('tm', 'heads'), may hold values from -6 to 6
- forward_out: bfloat16 [4096, 6144], P('tm', 'heads'), may hold values from -1.5 to 1.5
- out_grad: bfloat16 [4096, 6144], P('tm', 'heads'), may hold values from -6 to 6
- log_sums: float32 [48, 4096], P('heads', 'tm')
- group_index: int32 [4096], replicated, may hold values from 0 to 63, never falling along the last dimension, each value on 1 to 128 neighbouring positions
- query_gain: float32 [6144], P('heads'), may hold values from 0.5 to 1.5
- key_gain: float32 [6144], P('heads'), may hold values from 0.5 to 1.5
Outputs:
- query_grad: bfloat16 [4096, 6144], P('tm', 'heads')
- key_grad: bfloat16 [4096, 6144], P('tm', 'heads')
- values_grad: bfloat16 [4096, 6144], P('tm', 'heads')
The draws below stay inside these ranges and needn't reach their ends.
Inputs may be any that keep to these rules, and one draw needn't show every extreme that they name: `group_index`: group numbers never fall along the sequence; each group holds 1 to 128 tokens and one holds exactly 128.
All inputs are finite; a program needn't handle non-finite values.
Results may differ from the reference program's by a relative error of at most 0.012.
The reference program's roundings to bfloat16 on the way count: a program that leaves them out, or rounds other values in their place, can miss the bound.
Values may be sent and summed in bfloat16 or wider, within the bound.
A program may use at most 128 MiB of HBM per device.

```python
import math
import jax
import jax.numpy as jnp
import numpy as np
from jax import lax

D = 6144
HEADS = 48
HEAD_DIM = 128
TOK_DEV = 128
TOKENS = 4096
GROUPS = 64


def scaled_rows(entries, key, rise):
    row_factor = jnp.exp(jax.random.uniform(key, (TOKENS, 1), jnp.float32, 0.0, math.log(10.0)))
    column_factor = jnp.power(rise, jnp.arange(D, dtype=jnp.float32) / D)
    return entries * row_factor * column_factor[None, :]


def draw_query_raw(key, part):
    key = jax.random.fold_in(key, 11)
    first, second = jax.random.split(key)
    entries = jnp.clip(jax.random.normal(first, (TOKENS, D), jnp.float32), -4.5, 4.5)
    return scaled_rows(entries, second, 1.732).astype(jnp.bfloat16)


def draw_key_raw(key, part):
    key = jax.random.fold_in(key, 23)
    first, second = jax.random.split(key)
    entries = jnp.clip(jax.random.normal(first, (TOKENS, D), jnp.float32), -4.5, 4.5)
    return scaled_rows(entries, second, 1.732).astype(jnp.bfloat16)


def draw_log_sums(key, part):
    key = jax.random.fold_in(key, 37)
    position = jnp.arange(TOKENS, dtype=jnp.float32)
    base = 0.5 * jnp.log(position + 1.0 + TOK_DEV)[None, :]
    offset = jax.random.uniform(key, (HEADS, TOKENS), jnp.float32, 0.5, 1.5)
    return base + offset


def shard_levels(own_key, shape, pieces, least, largest):
    level = 1.0
    for dim, parts in pieces:
        draws = jax.random.uniform(jax.random.fold_in(jax.random.fold_in(own_key, 6), dim), (parts,), jnp.float32, least / len(pieces), largest / len(pieces))
        level = level * jnp.repeat(jnp.exp(draws), shape[dim] // parts).reshape((-1,) + (1,) * (len(shape) - 1 - dim))
    return level


def split_up(count, total, bound, slope):
    weights = [(1 << 20) // math.isqrt(standing ** slope) + 1 for standing in range(2, count + 1)]
    spare, counts = total - bound - (count - 1), [1] * (count - 1)
    while spare > 0:
        free = [i for i in range(count - 1) if counts[i] < bound]
        whole, left = sum([weights[i] for i in free]), spare
        for i in free:
            addition = min(bound - counts[i], max(1, left * weights[i] // whole), spare)
            counts[i] = counts[i] + addition
            spare = spare - addition
    return np.array([bound] + counts)


def ragged(rng, number_of, total, bound, skew):
    if number_of == 2:
        one = jax.random.randint(rng, (), max(1, total - bound), min(bound, total - 1) + 1)
        return jnp.stack([one, total - one])
    tallies = jnp.asarray(split_up(number_of, total, bound, skew), jnp.int32)
    couples = (number_of - 1) // 2
    giver, sink = tallies[1:1 + 2 * couples:2], tallies[2:2 + 2 * couples:2]
    margin = jnp.minimum(giver - 1, bound - sink)
    shifted = jax.random.randint(jax.random.fold_in(rng, 1), (couples,), 0, 1 << 20) % (margin + 1)
    tallies = tallies.at[1:1 + 2 * couples:2].set(giver - shifted).at[2:2 + 2 * couples:2].set(sink + shifted)
    return tallies[jax.random.permutation(jax.random.fold_in(rng, 2), number_of)]


def gaussian(stream_key, dims, deviation, bound, cuts=(), held_as=jnp.bfloat16):
    gain = shard_levels(stream_key, dims, cuts, -0.22, 0.18) if cuts else 1.0
    drawn = jax.random.normal(stream_key, dims, jnp.float32) * deviation * gain
    return jnp.minimum(jnp.maximum(drawn, -bound), bound).astype(held_as)


def setup_inputs(seed: int = 0) -> dict:
    key_of = jax.random.split(jax.random.key(seed), 10)
    return {
        "query_raw": draw_query_raw(jax.random.fold_in(key_of[9], 71), 0),
        "key_raw": draw_key_raw(jax.random.fold_in(key_of[9], 71), 0),
        "values": gaussian(key_of[2], (TOKENS, D), 1.0, 6.0, ((0, 32), (1, 8))),
        "forward_out": gaussian(key_of[3], (TOKENS, D), 0.25, 1.5, ((0, 32), (1, 8))),
        "out_grad": gaussian(key_of[4], (TOKENS, D), 1.0, 6.0, ((0, 32), (1, 8))),
        "log_sums": draw_log_sums(jax.random.fold_in(key_of[9], 71), 0),
        "group_index": jnp.searchsorted(jnp.cumsum(ragged(key_of[6], GROUPS, TOKENS, TOK_DEV, 1)), jnp.arange(TOKENS), side="right").astype(jnp.int32),
        "query_gain": jnp.clip(1.0 + 0.1 * jax.random.normal(key_of[7], (D,), jnp.float32), 0.5, 1.5),
        "key_gain": jnp.clip(1.0 + 0.1 * jax.random.normal(key_of[8], (D,), jnp.float32), 0.5, 1.5),
    }


EPS = 1e-06

def reference(query_raw, key_raw, values, forward_out, out_grad, log_sums, group_index, query_gain, key_gain):
    query_float = query_raw.astype(jnp.float32)
    key_float = key_raw.astype(jnp.float32)
    query_scale = lax.rsqrt(lax.optimization_barrier(jnp.mean(query_float * query_float, axis=1)) + EPS)
    key_scale = lax.rsqrt(lax.optimization_barrier(jnp.mean(key_float * key_float, axis=1)) + EPS)
    query_norm = (query_float * query_scale[:, None] * query_gain).astype(jnp.bfloat16)
    key_norm = (key_float * key_scale[:, None] * key_gain).astype(jnp.bfloat16)
    allowed = group_index[None, :] <= group_index[:, None]
    score_scale = 1.0 / math.sqrt(HEAD_DIM)

    def split_heads(matrix):
        return matrix.reshape(TOKENS, HEADS, HEAD_DIM).transpose(1, 0, 2)

    def merge_heads(stacked):
        return stacked.transpose(1, 0, 2).reshape(TOKENS, D)

    def one_head(inputs):
        query_part, key_part, value_part, output_part, grad_part, head_sums = inputs
        scores = jnp.dot(query_part, key_part.T, preferred_element_type=jnp.float32) * score_scale
        probs = jnp.exp(jnp.where(allowed, scores - head_sums[:, None], -jnp.inf))
        out_dots = lax.optimization_barrier(jnp.sum(grad_part.astype(jnp.float32) * output_part.astype(jnp.float32), axis=1))
        dprobs = jnp.dot(grad_part, value_part.T, preferred_element_type=jnp.float32)
        dscores = (probs * (dprobs - out_dots[:, None])).astype(jnp.bfloat16)
        value_grads = jnp.dot(probs.astype(jnp.bfloat16).T, grad_part, preferred_element_type=jnp.float32)
        query_grads = jnp.dot(dscores, key_part, preferred_element_type=jnp.float32) * score_scale
        key_grads = jnp.dot(dscores.T, query_part, preferred_element_type=jnp.float32) * score_scale
        return (query_grads, key_grads, value_grads)
    query_grads, key_grads, value_grads = lax.map(one_head, (split_heads(query_norm), split_heads(key_norm), split_heads(values), split_heads(forward_out), split_heads(out_grad), log_sums))
    query_dnorm = merge_heads(query_grads) * query_gain
    key_dnorm = merge_heads(key_grads) * key_gain
    query_dot = lax.optimization_barrier(jnp.sum(query_float * query_dnorm, axis=1))
    key_dot = lax.optimization_barrier(jnp.sum(key_float * key_dnorm, axis=1))
    query_grad = query_scale[:, None] * query_dnorm - query_float * (query_scale * query_scale * query_scale * query_dot / D)[:, None]
    key_grad = key_scale[:, None] * key_dnorm - key_float * (key_scale * key_scale * key_scale * key_dot / D)[:, None]
    return (query_grad.astype(jnp.bfloat16), key_grad.astype(jnp.bfloat16), merge_heads(value_grads).astype(jnp.bfloat16))
```

```python
import functools
import math

import jax
import jax.numpy as jnp
from jax import lax
from jax.experimental import pallas as pl
from jax.experimental.pallas import tpu as pltpu
from jax.sharding import PartitionSpec as P

D = 6144
HEAD_DIM = 128
EPS = 1e-06
WIN = 128
HERE = 6
WINDOWS = 32
CHUNK = 512
MESH = pl.DeviceIdType.MESH
F32 = jnp.float32
BF16 = jnp.bfloat16
LOG2E = math.log2(math.e)
SCORE_SCALE = 1.0 / math.sqrt(HEAD_DIM)
NT = (((1,), (1,)), ((), ()))
NN = (((1,), (0,)), ((), ()))


def dot(a, b, dims):
    return lax.dot_general(a, b, dims, preferred_element_type=F32)


def worker_chip(wid):
    x = wid // 3
    y = (x + 1 + wid % 3) % 4
    return 4 * x + y


def lanes_to_row(block):
    return jnp.sum(block.T, axis=0, keepdims=True)


def row_to_lanes(row):
    return jnp.broadcast_to(row, (WIN, WIN)).T


def kernel(
    q_hbm, k_hbm, v_hbm, fo_hbm, do_hbm, ls_ref, grp_ref, qg_ref, kg_ref,
    qgrad_ref, kgrad_ref, vgrad_ref,
    qraw, kraw, vraw, foraw, doraw, qn, kn, scq, sck,
    kv, qd, stats, st_src, zs, zx, acc, accq, kt, dqout, sib_out, sib_in, kvout,
    dqr, dkvr, qdn, kdn,
    load_sem, z_send, z_recv, sk, sv, sq, sd, ss, kv_recv, fwd_send, fwd_recv,
    qd_recv, st_recv, dq_send, dq_recv, sib_send, sib_recv, kvs, dkv_recv,
):
    t = lax.axis_index("tm")
    z = lax.axis_index("heads")
    chip = t // 2
    core = t % 2
    sibling = t + 1 - 2 * core
    cx = chip // 4
    cr = (chip % 4 - cx + 3) % 4
    is_worker = cr != 3
    wid = 3 * cx + cr
    head = wid // 2
    par = wid % 2

    loads = [
        pltpu.make_async_copy(src, dst, load_sem.at[i])
        for i, (src, dst) in enumerate(
            ((q_hbm, qraw), (k_hbm, kraw), (do_hbm, doraw), (fo_hbm, foraw), (v_hbm, vraw))
        )
    ]
    for c in loads:
        c.start()
    barrier = pltpu.get_barrier_semaphore()

    def greet_tm(i, _):
        pl.semaphore_signal(barrier, inc=1, device_id={"tm": (t + i) % WINDOWS}, device_id_type=MESH)
        return 0

    def greet_z(i, _):
        pl.semaphore_signal(barrier, inc=1, device_id={"heads": (z + i) % 8}, device_id_type=MESH)
        return 0

    lax.fori_loop(1, 8, greet_z, 0)
    lax.fori_loop(1, WINDOWS, greet_tm, 0)

    def cols(h):
        return slice(h * HEAD_DIM, (h + 1) * HEAD_DIM)

    loads[0].wait()
    loads[1].wait()
    zs[...] = jnp.zeros_like(zs)
    for row, raw in ((0, qraw), (1, kraw)):
        total = jnp.zeros((WIN, WIN), F32)
        for h in range(HERE):
            x = raw[:, cols(h)].astype(F32)
            total = total + x * x
        zs[0, row : row + 1, :] = lanes_to_row(total)

    loads[2].wait()
    loads[3].wait()
    own = grp_ref[pl.ds(t, 1), :].astype(F32)
    nxt = grp_ref[pl.ds(jnp.minimum(t + 1, WINDOWS - 1), 1), :].astype(F32)
    seen = (row_to_lanes(own) <= own).astype(F32)
    seen_next = jnp.where(
        (t < WINDOWS - 1) & (row_to_lanes(nxt) <= own), 1.0, 0.0
    )
    last = (t * WIN - 1).astype(F32) + jnp.sum(seen + seen_next, axis=0, keepdims=True)
    st_src[...] = jnp.zeros_like(st_src)
    for h in range(HERE):
        prod = doraw[:, cols(h)].astype(F32) * foraw[:, cols(h)].astype(F32)
        st_src[h, 0:1, :] = ls_ref[h : h + 1, :] * LOG2E
        st_src[h, 1:2, :] = lanes_to_row(prod)
        st_src[h, 2:3, :] = last
    loads[4].wait()

    pl.semaphore_wait(barrier, WINDOWS - 1 + 7)

    def exchange_z(which):
        def send(i, _):
            pltpu.make_async_remote_copy(
                src_ref=zs.at[which], dst_ref=zx.at[which, z],
                send_sem=z_send.at[which, i], recv_sem=z_recv.at[which],
                device_id={"heads": (z + i) % 8}, device_id_type=MESH,
            ).start()
            return 0

        lax.fori_loop(1, 8, send, 0)
        zx[which, pl.ds(z, 1)] = zs[pl.ds(which, 1)]

    def exchange_z_wait(which):
        part = zx.at[which, pl.ds(0, 7)]
        pltpu.make_async_copy(part, part, z_recv.at[which]).wait()
        return jnp.sum(zx[which], axis=0)

    exchange_z(0)

    def put(src, dst, send_sem, recv_sem, target):
        @pl.when(target == t)
        def _():
            pltpu.make_async_copy(src, dst, recv_sem).start()

        @pl.when(target != t)
        def _():
            pltpu.make_async_remote_copy(
                src_ref=src, dst_ref=dst, send_sem=send_sem, recv_sem=recv_sem,
                device_id={"tm": target}, device_id_type=MESH,
            ).start()

    def put_wait(src, send_sem, target):
        @pl.when(target != t)
        def _():
            pltpu.make_async_copy(src, src, send_sem).wait()

    own_par = t % 2
    own_slot = t // 2
    own_pair = t // 4
    own_core = (t // 2 + t // 4) % 2
    first = (t * HERE) // WINDOWS

    def head_cols(h):
        return pl.ds(pl.multiple_of(h * HEAD_DIM, HEAD_DIM), HEAD_DIM)

    def key_target(h, which):
        return 2 * worker_chip(2 * h + own_par) + which

    def query_target(h, which):
        return 2 * worker_chip(2 * h + which) + own_core

    def send_keys(src, which, sems):
        def step(i, _):
            h = (first + i) % HERE
            put(
                src.at[:, head_cols(h)],
                kv.at[which, pl.ds(pl.multiple_of(own_slot * WIN, WIN), WIN), :],
                sems.at[h], kv_recv, key_target(h, which),
            )
            return 0

        lax.fori_loop(0, HERE, step, 0)

    def send_queries(src, which, sems):
        def step(i, _):
            h = ((first + i // 2) % HERE)
            to = i % 2
            put(
                src.at[:, head_cols(h)],
                qd.at[own_pair, which, pl.ds(pl.multiple_of(own_par * WIN, WIN), WIN), :],
                sems.at[h, to], qd_recv.at[own_pair], query_target(h, to),
            )
            return 0

        lax.fori_loop(0, 2 * HERE, step, 0)

    def send_stats():
        def step(i, _):
            h = ((first + i // 2) % HERE)
            to = i % 2
            put(
                st_src.at[h],
                stats.at[own_pair, :, pl.ds(pl.multiple_of(own_par * WIN, WIN), WIN)],
                ss.at[h, to], st_recv.at[own_pair], query_target(h, to),
            )
            return 0

        lax.fori_loop(0, 2 * HERE, step, 0)

    send_keys(vraw, 1, sv)
    send_stats()
    send_queries(doraw, 1, sd)

    totals = exchange_z_wait(0)
    scales = lax.rsqrt(totals / D + EPS)
    scq[...] = row_to_lanes(scales[0:1, :])
    sck[...] = row_to_lanes(scales[1:2, :])
    for h in range(HERE):
        kn[:, cols(h)] = (kraw[:, cols(h)].astype(F32) * sck[...] * kg_ref[:, cols(h)]).astype(BF16)
    send_keys(kn, 0, sk)
    for h in range(HERE):
        qn[:, cols(h)] = (qraw[:, cols(h)].astype(F32) * scq[...] * qg_ref[:, cols(h)]).astype(BF16)
    send_queries(qn, 0, sq)

    @pl.when(is_worker)
    def _():
        acc[...] = jnp.zeros_like(acc)
        mine = kv.at[core]
        pltpu.make_async_copy(mine, mine, kv_recv).wait()
        forward = pltpu.make_async_remote_copy(
            src_ref=kv.at[core], dst_ref=kv.at[core], send_sem=fwd_send, recv_sem=fwd_recv,
            device_id={"tm": sibling}, device_id_type=MESH,
        )
        forward.start()
        forward.wait_recv()

        def turn(i, _):
            rows = pl.ds(pl.multiple_of(i * WIN, WIN), WIN)
            kt[:, rows] = kv[0, rows, :].T
            return 0

        lax.fori_loop(0, 16, turn, 0)
        start = ((head + 1) * 4) // 3 - 1

        def pair_step(i, _):
            m = (start - i + 8) % 8
            p = 2 * m + (core + m) % 2
            pltpu.make_async_copy(stats.at[m], stats.at[m], st_recv.at[m]).wait()
            pltpu.make_async_copy(qd.at[m], qd.at[m], qd_recv.at[m]).wait()
            accq[...] = jnp.zeros_like(accq)

            def chunk_step(c, _):
                rows = pl.ds(pl.multiple_of(c * CHUNK, CHUNK), CHUNK)
                q = qd[m, 0]
                do = qd[m, 1]
                s = dot(kv[0, rows, :], q, NT)
                probs = jnp.exp2(s * (SCORE_SCALE * LOG2E) - stats[m, 0:1, :])
                r = lax.broadcasted_iota(jnp.int32, (CHUNK, 2 * WIN), 0)
                place = (r + WIN * (r // WIN) + (c * 2 * CHUNK + par * WIN)).astype(F32)
                probs = jnp.where(place <= stats[m, 2:3, :], probs, 0.0)
                dp = dot(kv[1, rows, :], do, NT)
                ds = (probs * (dp - stats[m, 1:2, :])).astype(BF16)
                acc[1, rows, :] += dot(probs.astype(BF16), do, NN)
                acc[0, rows, :] += dot(ds, q, NN)
                accq[...] += dot(kt[:, rows], ds, NN)
                return 0

            steps = (jnp.minimum((p + 2) * WIN, 2048) + CHUNK - 1) // CHUNK
            lax.fori_loop(0, steps, chunk_step, 0)
            dqout[m] = accq[...].T.astype(BF16)

            def back(j, _):
                put(
                    dqout.at[m, pl.ds(pl.multiple_of(j * WIN, WIN), WIN), :],
                    dqr.at[head, par], dq_send.at[m, j], dq_recv, 2 * p + j,
                )
                return 0

            lax.fori_loop(0, 2, back, 0)
            return 0

        lax.fori_loop(0, 8, pair_step, 0)

        sib_out[...] = acc[1 - core].astype(BF16)
        swap = pltpu.make_async_remote_copy(
            src_ref=sib_out, dst_ref=sib_in, send_sem=sib_send, recv_sem=sib_recv,
            device_id={"tm": sibling}, device_id_type=MESH,
        )
        swap.start()
        swap.wait_recv()
        kvout[...] = (acc[core] + sib_in[...].astype(F32)).astype(BF16)

        def back(i, _):
            put(
                kvout.at[pl.ds(pl.multiple_of(i * WIN, WIN), WIN), :],
                dkvr.at[core, head], kvs.at[i], dkv_recv.at[core], 2 * i + par,
            )
            return 0

        lax.fori_loop(0, 16, back, 0)
        forward.wait_send()
        swap.wait_send()

        def back_wait(i, _):
            put_wait(kvout.at[pl.ds(0, WIN), :], kvs.at[i], 2 * i + par)
            return 0

        lax.fori_loop(0, 16, back_wait, 0)

        def dq_wait(i, _):
            m = i // 2
            put_wait(
                dqout.at[0, pl.ds(0, WIN), :], dq_send.at[m, i % 2],
                2 * (2 * m + (core + m) % 2) + i % 2,
            )
            return 0

        lax.fori_loop(0, 16, dq_wait, 0)

    pltpu.make_async_copy(dqr, dqr, dq_recv).wait()
    part = jnp.zeros((WIN, WIN), F32)
    for h in range(HERE):
        d = (dqr[h, 0].astype(F32) + dqr[h, 1].astype(F32)) * SCORE_SCALE * qg_ref[:, cols(h)]
        qdn[:, cols(h)] = d
        part = part + qraw[:, cols(h)].astype(F32) * d
    zs[1, 0:1, :] = lanes_to_row(part)
    pltpu.make_async_copy(dkvr.at[0], dkvr.at[0], dkv_recv.at[0]).wait()
    part = jnp.zeros((WIN, WIN), F32)
    for h in range(HERE):
        d = dkvr[0, h].astype(F32) * SCORE_SCALE * kg_ref[:, cols(h)]
        kdn[:, cols(h)] = d
        part = part + kraw[:, cols(h)].astype(F32) * d
    zs[1, 1:2, :] = lanes_to_row(part)
    exchange_z(1)
    pltpu.make_async_copy(dkvr.at[1], dkvr.at[1], dkv_recv.at[1]).wait()
    for h in range(HERE):
        vgrad_ref[:, cols(h)] = dkvr[1, h]
    dots = exchange_z_wait(1) / D
    cq = row_to_lanes(dots[0:1, :])
    ck = row_to_lanes(dots[1:2, :])
    for sc, cc, raw, dn, out in (
        (scq, cq, qraw, qdn, qgrad_ref), (sck, ck, kraw, kdn, kgrad_ref),
    ):
        s = sc[...]
        coef = s * s * s * cc
        for h in range(HERE):
            out[:, cols(h)] = (s * dn[:, cols(h)] - raw[:, cols(h)].astype(F32) * coef).astype(BF16)

    def z_wait(i, _):
        for which in range(2):
            pltpu.make_async_copy(zs.at[which], zs.at[which], z_send.at[which, i]).wait()
        return 0

    lax.fori_loop(1, 8, z_wait, 0)
    block = kn.at[:, pl.ds(0, HEAD_DIM)]

    def send_wait(h, _):
        put_wait(block, sk.at[h], key_target(h, 0))
        put_wait(block, sv.at[h], key_target(h, 1))
        for to in range(2):
            put_wait(block, sq.at[h, to], query_target(h, to))
            put_wait(block, sd.at[h, to], query_target(h, to))
            put_wait(st_src.at[0], ss.at[h, to], query_target(h, to))
        return 0

    lax.fori_loop(0, HERE, send_wait, 0)


def on_device(q, k, v, fo, do, log_sums, group_index, q_gain, k_gain):
    block = (WIN, HERE * HEAD_DIM)
    any_spec = pl.BlockSpec(memory_space=pl.ANY)
    vmem_spec = pl.BlockSpec(memory_space=pltpu.VMEM)
    dma = pltpu.SemaphoreType.DMA
    return pl.pallas_call(
        kernel,
        out_shape=[jax.ShapeDtypeStruct(block, BF16)] * 3,
        in_specs=[any_spec] * 5 + [vmem_spec] * 4,
        out_specs=[vmem_spec] * 3,
        scratch_shapes=[
            *[pltpu.VMEM(block, BF16)] * 7,
            pltpu.VMEM((WIN, WIN), F32),
            pltpu.VMEM((WIN, WIN), F32),
            pltpu.VMEM((2, 2048, HEAD_DIM), BF16),
            pltpu.VMEM((8, 2, 2 * WIN, HEAD_DIM), BF16),
            pltpu.VMEM((8, 8, 2 * WIN), F32),
            pltpu.VMEM((HERE, 8, WIN), F32),
            pltpu.VMEM((2, 8, WIN), F32),
            pltpu.VMEM((2, 8, 8, WIN), F32),
            pltpu.VMEM((2, 2048, HEAD_DIM), F32),
            pltpu.VMEM((HEAD_DIM, 2 * WIN), F32),
            pltpu.VMEM((HEAD_DIM, 2048), BF16),
            pltpu.VMEM((8, 2 * WIN, HEAD_DIM), BF16),
            pltpu.VMEM((2048, HEAD_DIM), BF16),
            pltpu.VMEM((2048, HEAD_DIM), BF16),
            pltpu.VMEM((2048, HEAD_DIM), BF16),
            pltpu.VMEM((HERE, 2, WIN, HEAD_DIM), BF16),
            pltpu.VMEM((2, HERE, WIN, HEAD_DIM), BF16),
            pltpu.VMEM(block, F32),
            pltpu.VMEM(block, F32),
            dma((5,)), dma((2, 8)), dma((2,)),
            dma((HERE,)), dma((HERE,)), dma((HERE, 2)), dma((HERE, 2)), dma((HERE, 2)),
            dma, dma, dma,
            dma((8,)), dma((8,)), dma((8, 2)), dma, dma, dma, dma((16,)), dma((2,)),
        ],
        compiler_params=pltpu.CompilerParams(
            collective_id=0, has_side_effects=True, vmem_limit_bytes=40 << 20
        ),
        cost_estimate=pl.CostEstimate(
            flops=2 * 10**9, bytes_accessed=2 * 10**6, transcendentals=2 * 10**6
        ),
    )(
        q, k, v, fo, do, log_sums, group_index.reshape(WINDOWS, WIN),
        q_gain.reshape(1, -1), k_gain.reshape(1, -1),
    )


def solution(mesh):
    tok, heads = P("tm", "heads"), P("heads")
    return jax.shard_map(
        on_device,
        mesh=mesh,
        in_specs=(tok, tok, tok, tok, tok, P("heads", "tm"), P(), heads, heads),
        out_specs=(tok, tok, tok),
        check_vma=False,
    )
```

```python
import functools
import math

import jax
import jax.numpy as jnp
from jax import lax
from jax.experimental import pallas as pl
from jax.experimental.pallas import tpu as pltpu
from jax.sharding import PartitionSpec as P

D = 6144
HEAD_DIM = 128
EPS = 1e-06
WIN = 128
HERE = 6
WINDOWS = 32
BLOCKS = WINDOWS // 2
KEYS = BLOCKS * WIN
LEAD = 4
WINDOW = 2
LAG = 2
PAIRS = 8
MESH = pl.DeviceIdType.MESH
F32 = jnp.float32
BF16 = jnp.bfloat16
LOG2E = math.log2(math.e)
SCORE_SCALE = 1.0 / math.sqrt(HEAD_DIM)
NT = (((1,), (1,)), ((), ()))
NN = (((1,), (0,)), ((), ()))


def dot(a, b, dims):
    return lax.dot_general(a, b, dims, preferred_element_type=F32)


def worker_at(x, y):
    turn = (y - x + 3) % 4
    middle = turn % 2
    head = middle * (4 + x // 2) + (1 - middle) * x
    part = middle * (1 - x % 2) + (1 - middle) * (1 - turn // 2)
    return turn != 3, head, part


def across(y, k):
    return (y // 2 + k // 2) % 2 * 2 + (y + k) % 2


def lanes_to_row(block):
    return jnp.sum(block.T, axis=0, keepdims=True)


def row_to_lanes(row):
    return jnp.broadcast_to(row, (WIN, WIN)).T


def kernel(
    q_hbm, k_hbm, v_hbm, fo_hbm, do_hbm, ls_hbm, grp_hbm, qg_hbm, kg_hbm,
    qgrad_ref, kgrad_ref, vgrad_ref,
    qraw, kraw, vraw, foraw, doraw, qn, scq, sck,
    kv, qd, stats, st_src, zs, zx, acc, accq, kt, dqout, sib_out, sib_in, kvout,
    dqr, dkvr, qdn, kdn,
    place, k_rows, kst_src, gains, spare16, spare32, ls_ref, grp_ref, qg_ref, kg_ref,
    load_sem, z_send, z_recv, sk, sv, sq, ss, sks, kst_recv, kv_recv, fwd_send, fwd_recv,
    qd_recv, st_recv, dq_send, dq_recv, sib_send, sib_recv, kvs, dkv_recv,
):
    t = lax.axis_index("tm")
    z = lax.axis_index("heads")
    chip = t // 2
    core = t % 2
    sibling = t + 1 - 2 * core
    cx = chip // 4
    cy = chip % 4
    is_worker, head, par = worker_at(cx, cy)

    loads = [
        pltpu.make_async_copy(src, dst, load_sem.at[i])
        for i, (src, dst) in enumerate(
            (
                (q_hbm, qraw), (k_hbm, kraw), (do_hbm, doraw), (fo_hbm, foraw), (v_hbm, vraw),
                (ls_hbm, ls_ref), (grp_hbm, grp_ref), (qg_hbm, qg_ref), (kg_hbm, kg_ref),
            )
        )
    ]
    for c in loads:
        c.start()
    barrier = pltpu.get_barrier_semaphore()

    def greet_tm(i, _):
        pl.semaphore_signal(barrier, inc=1, device_id={"tm": (t + i) % WINDOWS}, device_id_type=MESH)
        return 0

    def greet_z(i, _):
        pl.semaphore_signal(barrier, inc=1, device_id={"heads": (z + i) % 8}, device_id_type=MESH)
        return 0

    with jax.named_scope("greet"):
        lax.fori_loop(1, 8, greet_z, 0)
        lax.fori_loop(1, WINDOWS, greet_tm, 0)

    def cols(h):
        return slice(h * HEAD_DIM, (h + 1) * HEAD_DIM)

    def gain(ref, h):
        return ref[pl.ds(h * HEAD_DIM, HEAD_DIM)].reshape(1, HEAD_DIM)

    with jax.named_scope("sums"):
        loads[0].wait()
        loads[1].wait()
        zs[...] = jnp.zeros_like(zs)
        for row, raw in ((0, qraw), (1, kraw)):
            total = jnp.zeros((WIN, WIN), F32)
            for h in range(HERE):
                x = raw[:, cols(h)].astype(F32)
                total = total + x * x
            zs[0, row : row + 1, :] = lanes_to_row(total)

    with jax.named_scope("rowdata"):
        loads[2].wait()
        loads[3].wait()
        loads[5].wait()
        loads[6].wait()
        own = grp_ref[pl.ds(t, 1), :].astype(F32)
        nxt = grp_ref[pl.ds(jnp.minimum(t + 1, WINDOWS - 1), 1), :].astype(F32)
        seen = (row_to_lanes(own) <= own).astype(F32)
        seen_next = jnp.where(
            (t < WINDOWS - 1) & (row_to_lanes(nxt) <= own), 1.0, 0.0
        )
        last = (t * WIN - 1).astype(F32) + jnp.sum(seen + seen_next, axis=0, keepdims=True)
        st_src[...] = jnp.zeros_like(st_src)
        for h in range(HERE):
            prod = doraw[:, cols(h)].astype(F32) * foraw[:, cols(h)].astype(F32)
            st_src[h, 0:1, :] = ls_ref[h : h + 1, :] * LOG2E
            st_src[h, 1:2, :] = lanes_to_row(prod)
            st_src[h, 2:3, :] = last
        loads[4].wait()
        loads[7].wait()
        loads[8].wait()

    with jax.named_scope("meet"):
        pl.semaphore_wait(barrier, WINDOWS - 1 + 7)

    def exchange_z(which):
        def send(i, _):
            pltpu.make_async_remote_copy(
                src_ref=zs.at[which], dst_ref=zx.at[which, z],
                send_sem=z_send.at[which], recv_sem=z_recv.at[which],
                device_id={"heads": (z + i) % 8}, device_id_type=MESH,
            ).start()
            return 0

        lax.fori_loop(1, 8, send, 0)
        zx[which, pl.ds(z, 1)] = zs[pl.ds(which, 1)]

    def exchange_z_wait(which):
        part = zx.at[which, pl.ds(0, 7)]
        pltpu.make_async_copy(part, part, z_recv.at[which]).wait()
        return jnp.sum(zx[which], axis=0)

    exchange_z(0)

    def put(src, dst, send_sem, recv_sem, target, spare):
        @pl.when(target == t)
        def _():
            pltpu.make_async_copy(src, dst, recv_sem).start()
            pltpu.make_async_copy(src, spare, send_sem).start()

        @pl.when(target != t)
        def _():
            pltpu.make_async_remote_copy(
                src_ref=src, dst_ref=dst, send_sem=send_sem, recv_sem=recv_sem,
                device_id={"tm": target}, device_id_type=MESH,
            ).start()

    def wait_for(ref, sem):
        pltpu.make_async_copy(ref, ref, sem).wait()

    def rows_of(i, size=WIN):
        return pl.ds(pl.multiple_of(i * size, size), size)

    def head_cols(h):
        return pl.ds(pl.multiple_of(h * HEAD_DIM, HEAD_DIM), HEAD_DIM)

    own_part = t % 2
    own_slot = t // 2
    own_pair = t // 4
    own_core = (t // 2 + t // 4) % 2

    def for_workers(do):
        def step(i, _):
            x = (cx + i // 4) % 4
            y = (cy + i % 4) % 4
            there, h, part = worker_at(x, y)
            pl.when(there)(functools.partial(do, 2 * (4 * x + y), h, part))
            return 0

        lax.fori_loop(0, 16, step, 0)

    def send_keys(base, h, part):
        @pl.when(part == own_part)
        def _():
            for which, src, sem in ((0, kraw, sk), (1, vraw, sv)):
                put(
                    src.at[:, head_cols(h)], kv.at[which, rows_of(own_slot), :],
                    sem, kv_recv.at[own_slot // 2], base + which, spare16.at[which],
                )

    def send_rows(base, h, part):
        @pl.when(part == own_part)
        def _():
            put(kst_src, k_rows.at[own_slot], sks, kst_recv, base, spare32.at[0])

        put(
            st_src.at[h], stats.at[own_pair, :, rows_of(t % 2)],
            ss, st_recv, base + own_core, spare32.at[1],
        )

    def send_queries(base, h, part, sem):
        for which, src in ((1, doraw), (0, qn)):
            put(
                src.at[:, head_cols(h)], qd.at[own_pair, which, rows_of(t % 2), :],
                sem, qd_recv.at[own_pair], base + own_core, spare16.at[2 + which],
            )

    with jax.named_scope("send_kv"):
        for_workers(send_keys)

    with jax.named_scope("wait_z"):
        totals = exchange_z_wait(0)
    with jax.named_scope("send_q"):
        scales = lax.rsqrt(totals / D + EPS)
        kst_src[...] = scales
        for_workers(send_rows)
        scq[...] = row_to_lanes(scales[0:1, :])
        sck[...] = row_to_lanes(scales[1:2, :])
        for h in range(HERE):
            gains[h : h + 1, :] = gain(kg_ref, h)
            qn[:, cols(h)] = (qraw[:, cols(h)].astype(F32) * scq[...] * gain(qg_ref, h)).astype(BF16)


    def turn(j, do):
        for k in range(2):
            x = (cx + j // 2) % 4
            y = across(cy, 2 * (j % 2) + k)
            there, h, part = worker_at(x, y)
            pl.when(there)(functools.partial(do, 2 * (4 * x + y), h, part, sq.at[j, k]))

    def turn_sent(j, _):
        turn(j, lambda base, h, part, sem: wait_for(qd.at[0, 0], sem))
        return 0

    def send_turn(j, _):
        @pl.when(j >= WINDOW)
        def _():
            turn_sent(j - WINDOW, 0)

        turn(j, send_queries)
        return 0

    with jax.named_scope("hold"):
        wait_for(kraw, sk)
        wait_for(vraw, sv)
    with jax.named_scope("send_q0"):
        lax.fori_loop(0, jnp.where(is_worker, LEAD, PAIRS), send_turn, 0)

    @pl.when(is_worker)
    def _():
        with jax.named_scope("wait_kv"):
            acc[...] = jnp.zeros_like(acc)
            r = lax.broadcasted_iota(jnp.int32, (512, WIN), 0)
            place[...] = (r + WIN * (r // WIN)).astype(F32)

            @pl.when(core == 0)
            def _():
                wait_for(k_rows, kst_recv)

            def forward(c, _):
                piece = kv.at[core, rows_of(c, 256), :]
                wait_for(piece, kv_recv.at[c])

                @pl.when(core == 0)
                def _():
                    for j in range(2):
                        i = 2 * c + j
                        scale = row_to_lanes(k_rows[i, 1:2, :])
                        normed = kv[0, rows_of(i), :].astype(F32) * scale * gains[pl.ds(head, 1), :]
                        kv[0, rows_of(i), :] = normed.astype(BF16)

                pltpu.make_async_remote_copy(
                    src_ref=piece, dst_ref=piece, send_sem=fwd_send, recv_sem=fwd_recv.at[c],
                    device_id={"tm": sibling}, device_id_type=MESH,
                ).start()
                return 0

            lax.fori_loop(0, BLOCKS // 2, forward, 0)

        with jax.named_scope("forward"):

            def forwarded(c, _):
                rows = rows_of(c, 256)
                wait_for(kv.at[1 - core, rows, :], fwd_recv.at[c])
                kt[:, rows] = kv[0, rows, :].T
                return 0

            lax.fori_loop(0, BLOCKS // 2, forwarded, 0)
            wait_for(stats, st_recv)

        def give(c, _):
            sib_out[rows_of(c, 256), :] = acc[1 - core, rows_of(c, 256), :].astype(BF16)
            pltpu.make_async_remote_copy(
                src_ref=sib_out.at[rows_of(c, 256), :], dst_ref=sib_in.at[rows_of(c, 256), :],
                send_sem=sib_send, recv_sem=sib_recv.at[c],
                device_id={"tm": sibling}, device_id_type=MESH,
            ).start()
            return 0

        def finish(c, _):
            rows = rows_of(c, 256)
            pltpu.make_async_copy(sib_in.at[rows, :], sib_in.at[rows, :], sib_recv.at[c]).wait()
            kvout[rows, :] = (acc[core, rows, :] + sib_in[rows, :].astype(F32)).astype(BF16)
            for j in range(2):
                i = 2 * c + j
                put(
                    kvout.at[rows_of(i), :], dkvr.at[core, head],
                    kvs, dkv_recv.at[core], 2 * i + par, spare16.at[5],
                )
            return 0

        def row_of(i):
            return (cx - i // 2 + 4) % 4

        def pair_of(i):
            return 2 * row_of(i) + (cy // 2 + i) % 2

        def done_after(i):
            r = row_of(i)
            ready = ((r > cx) | (cx == 3)).astype(jnp.int32) * (i % 2)
            end = i // (PAIRS - 1)
            lo = ready * (1 - end) * (2 * r + 1 - par)
            hi = ready * jnp.minimum(2 * r + 3 - par, BLOCKS // 2)
            return lo, hi

        def finish_all(lo, hi):
            count = jnp.maximum(hi - lo, 1)
            lax.fori_loop(lo, hi, lambda c, _: finish(lo + (c - lo + 2 * cx) % count, _), 0)

        def pair_step(i, _):
            m = pair_of(i)

            @pl.when(i + LEAD < PAIRS)
            def _():
                send_turn(i + LEAD, 0)

            p = 2 * m + (core + m) % 2
            with jax.named_scope("wait_qd"):
                wait_for(qd.at[m], qd_recv.at[m])
            accq[...] = jnp.zeros_like(accq)

            def work(row, size, edge):
                rows = pl.ds(pl.multiple_of(row, 256), size)
                q = qd[m, 0]
                do = qd[m, 1]
                s = dot(kv[0, rows, :], q, NT)
                probs = jnp.exp2(s * (SCORE_SCALE * LOG2E) - stats[m, 0:1, :])
                if edge:
                    limit = stats[m, 2:3, :] - (2 * row + par * WIN).astype(F32)
                    at = place[:size, :]
                    probs = jnp.where(jnp.concatenate([at, at], axis=1) <= limit, probs, 0.0)
                dp = dot(kv[1, rows, :], do, NT)
                ds = (probs * (dp - stats[m, 1:2, :])).astype(BF16)
                acc[1, rows, :] += dot(probs.astype(BF16), do, NN)
                acc[0, rows, :] += dot(ds, q, NN)
                accq[...] += dot(kt[:, rows], ds, NN)

            chunks = jnp.minimum((p + 3 - par) // 2, BLOCKS // 2)
            inner = p // 4 * 2
            rest = chunks - inner

            def whole(c, _):
                work(c * 1024, 1024, False)
                return 0

            with jax.named_scope("chunks"):
                lax.fori_loop(0, inner // 4, whole, 0)

                @pl.when(inner % 4 == 2)
                def _():
                    work(inner // 4 * 1024, 512, False)

                @pl.when(rest >= 2)
                def _():
                    work(inner * 256, 512, True)

                @pl.when(rest % 2 == 1)
                def _():
                    work((chunks - 1) * 256, 256, True)

            dqout[m] = accq[...].T.astype(BF16)

            def back(j, _):
                put(
                    dqout.at[m, rows_of(j), :], dqr.at[par, head],
                    dq_send, dq_recv.at[par], 2 * p + j, spare16.at[4],
                )
                return 0

            lax.fori_loop(0, 2, back, 0)
            lax.fori_loop(*done_after(i), give, 0)

            @pl.when(i > LAG - 1)
            def _():
                finish_all(*done_after(i - LAG))

            return 0

        lax.fori_loop(0, PAIRS, pair_step, 0)
        with jax.named_scope("swap"):
            for i in range(PAIRS - LAG, PAIRS):
                finish_all(*done_after(i))

        with jax.named_scope("worker_waits"):

            wait_for(kv.at[0], fwd_send)
            wait_for(sib_out, sib_send)
            wait_for(kvout, kvs)
            wait_for(dqout, dq_send)

    with jax.named_scope("wait_dq"):
        for i in range(2):
            wait_for(dqr.at[i], dq_recv.at[i])

    part = jnp.zeros((WIN, WIN), F32)
    for h in range(HERE):
        d = (dqr[0, h].astype(F32) + dqr[1, h].astype(F32)) * SCORE_SCALE * gain(qg_ref, h)
        qdn[:, cols(h)] = d
        part = part + qraw[:, cols(h)].astype(F32) * d
    zs[1, 0:1, :] = lanes_to_row(part)
    with jax.named_scope("wait_dk"):
        pltpu.make_async_copy(dkvr.at[0], dkvr.at[0], dkv_recv.at[0]).wait()
    part = jnp.zeros((WIN, WIN), F32)
    for h in range(HERE):
        d = dkvr[0, h].astype(F32) * SCORE_SCALE * gain(kg_ref, h)
        kdn[:, cols(h)] = d
        part = part + kraw[:, cols(h)].astype(F32) * d
    zs[1, 1:2, :] = lanes_to_row(part)
    exchange_z(1)
    with jax.named_scope("wait_dv"):
        pltpu.make_async_copy(dkvr.at[1], dkvr.at[1], dkv_recv.at[1]).wait()
    for h in range(HERE):
        vgrad_ref[:, cols(h)] = dkvr[1, h]
    with jax.named_scope("wait_z2"):
        dots = exchange_z_wait(1) / D
    with jax.named_scope("final"):
        cq = row_to_lanes(dots[0:1, :])
        ck = row_to_lanes(dots[1:2, :])
        for sc, cc, raw, dn, out in (
            (scq, cq, qraw, qdn, qgrad_ref), (sck, ck, kraw, kdn, kgrad_ref),
        ):
            s = sc[...]
            coef = s * s * s * cc
            for h in range(HERE):
                out[:, cols(h)] = (
                    s * dn[:, cols(h)] - raw[:, cols(h)].astype(F32) * coef
                ).astype(BF16)

    with jax.named_scope("ends"):

        for which in range(2):
            wait_for(zx.at[which, pl.ds(0, 7)], z_send.at[which])
        wait_for(st_src, sks)
        lax.fori_loop(PAIRS - WINDOW, PAIRS, turn_sent, 0)
        wait_for(stats.at[pl.ds(0, 6)], ss)


def on_device(q, k, v, fo, do, log_sums, group_index, q_gain, k_gain):
    block = (WIN, HERE * HEAD_DIM)
    any_spec = pl.BlockSpec(memory_space=pl.ANY)
    vmem_spec = pl.BlockSpec(memory_space=pltpu.VMEM)
    dma = pltpu.SemaphoreType.DMA
    return pl.pallas_call(
        kernel,
        out_shape=[pltpu.VMEM(block, BF16)] * 3,
        in_specs=[any_spec] * 9,
        out_specs=[vmem_spec] * 3,
        scratch_shapes=[
            *[pltpu.VMEM(block, BF16)] * 6,
            pltpu.VMEM((WIN, WIN), F32),
            pltpu.VMEM((WIN, WIN), F32),
            pltpu.VMEM((2, KEYS, HEAD_DIM), BF16),
            pltpu.VMEM((8, 2, 2 * WIN, HEAD_DIM), BF16),
            pltpu.VMEM((8, 8, 2 * WIN), F32),
            pltpu.VMEM((HERE, 8, WIN), F32),
            pltpu.VMEM((2, 8, WIN), F32),
            pltpu.VMEM((2, 8, 8, WIN), F32),
            pltpu.VMEM((2, KEYS, HEAD_DIM), F32),
            pltpu.VMEM((HEAD_DIM, 2 * WIN), F32),
            pltpu.VMEM((HEAD_DIM, KEYS), BF16),
            pltpu.VMEM((8, 2 * WIN, HEAD_DIM), BF16),
            pltpu.VMEM((KEYS, HEAD_DIM), BF16),
            pltpu.VMEM((KEYS, HEAD_DIM), BF16),
            pltpu.VMEM((KEYS, HEAD_DIM), BF16),
            pltpu.VMEM((2, HERE, WIN, HEAD_DIM), BF16),
            pltpu.VMEM((2, HERE, WIN, HEAD_DIM), BF16),
            pltpu.VMEM(block, F32),
            pltpu.VMEM(block, F32),
            pltpu.VMEM((512, WIN), F32),
            pltpu.VMEM((BLOCKS, 8, WIN), F32),
            pltpu.VMEM((8, WIN), F32),
            pltpu.VMEM((8, WIN), F32),
            pltpu.VMEM((6, WIN, HEAD_DIM), BF16),
            pltpu.VMEM((2, 8, WIN), F32),
            pltpu.VMEM((HERE, WIN), F32),
            pltpu.VMEM((WINDOWS, WIN), jnp.int32),
            pltpu.VMEM((HERE * HEAD_DIM,), F32),
            pltpu.VMEM((HERE * HEAD_DIM,), F32),
            dma((9,)), dma((2,)), dma((2,)),
            dma, dma, dma((PAIRS, 2)), dma, dma,
            dma, dma((BLOCKS // 2,)), dma, dma((BLOCKS // 2,)),
            dma((8,)), dma, dma, dma((2,)), dma, dma((BLOCKS // 2,)),
            dma, dma((2,)),
        ],
        compiler_params=pltpu.CompilerParams(
            collective_id=0, has_side_effects=True, vmem_limit_bytes=60 << 20
        ),
        cost_estimate=pl.CostEstimate(
            flops=2 * 10**9, bytes_accessed=2 * 10**6, transcendentals=2 * 10**6
        ),
    )(
        q, k, v, fo, do, log_sums, group_index.reshape(WINDOWS, WIN),
        q_gain, k_gain,
    )


def solution(mesh):
    tok, heads = P("tm", "heads"), P("heads")
    return jax.shard_map(
        on_device,
        mesh=mesh,
        in_specs=(tok, tok, tok, tok, tok, P("heads", "tm"), P(), heads, heads),
        out_specs=(tok, tok, tok),
        check_vma=False,
    )
```

```python
import functools
import math

import jax
import jax.numpy as jnp
from jax import lax
from jax.experimental import pallas as pl
from jax.experimental.pallas import tpu as pltpu
from jax.sharding import PartitionSpec as P

D = 6144
HEAD_DIM = 128
EPS = 1e-06
WIN = 128
HERE = 6
WINDOWS = 32
BLOCKS = WINDOWS // 2
KEYS = BLOCKS * WIN
LEAD = 5
WINDOW = 4
LAG = 2
PAIRS = 8
MESH = pl.DeviceIdType.MESH
F32 = jnp.float32
BF16 = jnp.bfloat16
LOG2E = math.log2(math.e)
SCORE_SCALE = 1.0 / math.sqrt(HEAD_DIM)
NT = (((1,), (1,)), ((), ()))
NN = (((1,), (0,)), ((), ()))


def dot(a, b, dims):
    return lax.dot_general(a, b, dims, preferred_element_type=F32)


def worker_at(x, y):
    turn = (y - x + 3) % 4
    middle = turn % 2
    head = middle * (4 + x // 2) + (1 - middle) * x
    part = middle * (1 - x % 2) + (1 - middle) * (1 - turn // 2)
    return turn != 3, head, part


def across(y, k):
    return (y // 2 + k // 2) % 2 * 2 + (y + k) % 2


def lanes_to_row(block):
    return jnp.sum(block.T, axis=0, keepdims=True)


def row_to_lanes(row):
    return jnp.broadcast_to(row, (WIN, WIN)).T


def kernel(
    q_hbm, k_hbm, v_hbm, fo_hbm, do_hbm, ls_hbm, grp_hbm, qg_hbm, kg_hbm,
    grads_ref,
    qraw, kraw, vraw, foraw, doraw, qn, scq, sck,
    kv, qd, stats, st_src, zs, zx, acc, accq, kt, dqout, sib_out, sib_in, kvout,
    dqr, dkvr, qdn, kdn,
    place, k_rows, kst_src, gains, spare16, spare32, ls_ref, grp_ref, qg_ref, kg_ref,
    load_sem, z_send, z_recv, sk, sv, sq, ss, sks, kst_recv, kv_recv, fwd_send, fwd_recv,
    qd_recv, st_recv, dq_send, dq_recv, sib_send, sib_recv, kvs, dkv_recv,
):
    t = lax.axis_index("tm")
    z = lax.axis_index("heads")
    chip = t // 2
    core = t % 2
    sibling = t + 1 - 2 * core
    cx = chip // 4
    cy = chip % 4
    is_worker, head, par = worker_at(cx, cy)

    loads = [
        pltpu.make_async_copy(src, dst, load_sem.at[i])
        for i, (src, dst) in enumerate(
            (
                (q_hbm, qraw), (k_hbm, kraw), (do_hbm, doraw), (fo_hbm, foraw), (v_hbm, vraw),
                (ls_hbm, ls_ref), (grp_hbm, grp_ref), (qg_hbm, qg_ref), (kg_hbm, kg_ref),
            )
        )
    ]
    for c in loads:
        c.start()
    barrier = pltpu.get_barrier_semaphore()

    def greet_tm(i, _):
        pl.semaphore_signal(barrier, inc=1, device_id={"tm": (t + i) % WINDOWS}, device_id_type=MESH)
        return 0

    def greet_z(i, _):
        pl.semaphore_signal(barrier, inc=1, device_id={"heads": (z + i) % 8}, device_id_type=MESH)
        return 0

    with jax.named_scope("greet"):
        lax.fori_loop(1, 8, greet_z, 0)
        lax.fori_loop(1, WINDOWS, greet_tm, 0)

    def cols(h):
        return slice(h * HEAD_DIM, (h + 1) * HEAD_DIM)

    def gain(ref, h):
        return ref[pl.ds(h * HEAD_DIM, HEAD_DIM)].reshape(1, HEAD_DIM)

    with jax.named_scope("sums"):
        loads[0].wait()
        loads[1].wait()
        zs[...] = jnp.zeros_like(zs)
        for row, raw in ((0, qraw), (1, kraw)):
            total = jnp.zeros((WIN, WIN), F32)
            for h in range(HERE):
                x = raw[:, cols(h)].astype(F32)
                total = total + x * x
            zs[0, row : row + 1, :] = lanes_to_row(total)

    with jax.named_scope("rowdata"):
        loads[2].wait()
        loads[3].wait()
        loads[5].wait()
        loads[6].wait()
        own = grp_ref[pl.ds(t, 1), :].astype(F32)
        nxt = grp_ref[pl.ds(jnp.minimum(t + 1, WINDOWS - 1), 1), :].astype(F32)
        seen = (row_to_lanes(own) <= own).astype(F32)
        seen_next = jnp.where(
            (t < WINDOWS - 1) & (row_to_lanes(nxt) <= own), 1.0, 0.0
        )
        last = (t * WIN - 1).astype(F32) + jnp.sum(seen + seen_next, axis=0, keepdims=True)
        st_src[...] = jnp.zeros_like(st_src)
        for h in range(HERE):
            prod = doraw[:, cols(h)].astype(F32) * foraw[:, cols(h)].astype(F32)
            st_src[h, 0:1, :] = ls_ref[h : h + 1, :] * LOG2E
            st_src[h, 1:2, :] = lanes_to_row(prod)
            st_src[h, 2:3, :] = last
        loads[4].wait()
        loads[7].wait()
        loads[8].wait()

    with jax.named_scope("meet"):
        pl.semaphore_wait(barrier, WINDOWS - 1 + 7)

    def exchange_z(which):
        def send(i, _):
            pltpu.make_async_remote_copy(
                src_ref=zs.at[which], dst_ref=zx.at[which, z],
                send_sem=z_send.at[which], recv_sem=z_recv.at[which],
                device_id={"heads": (z + i) % 8}, device_id_type=MESH,
            ).start()
            return 0

        lax.fori_loop(1, 8, send, 0)
        zx[which, pl.ds(z, 1)] = zs[pl.ds(which, 1)]

    def exchange_z_wait(which):
        part = zx.at[which, pl.ds(0, 7)]
        pltpu.make_async_copy(part, part, z_recv.at[which]).wait()
        return jnp.sum(zx[which], axis=0)

    exchange_z(0)

    def put(src, dst, send_sem, recv_sem, target, spare):
        @pl.when(target == t)
        def _():
            pltpu.make_async_copy(src, dst, recv_sem).start()
            pltpu.make_async_copy(src, spare, send_sem).start()

        @pl.when(target != t)
        def _():
            pltpu.make_async_remote_copy(
                src_ref=src, dst_ref=dst, send_sem=send_sem, recv_sem=recv_sem,
                device_id={"tm": target}, device_id_type=MESH,
            ).start()

    def wait_for(ref, sem):
        pltpu.make_async_copy(ref, ref, sem).wait()

    def rows_of(i, size=WIN):
        return pl.ds(pl.multiple_of(i * size, size), size)

    def head_cols(h):
        return pl.ds(pl.multiple_of(h * HEAD_DIM, HEAD_DIM), HEAD_DIM)

    own_part = t % 2
    own_slot = t // 2
    own_pair = t // 4
    own_core = (t // 2 + t // 4) % 2

    def for_workers(do):
        def step(i, _):
            x = (cx + i // 4) % 4
            y = (cy + i % 4) % 4
            there, h, part = worker_at(x, y)
            pl.when(there)(functools.partial(do, 2 * (4 * x + y), h, part))
            return 0

        lax.fori_loop(0, 16, step, 0)

    def send_keys(base, h, part):
        @pl.when(part == own_part)
        def _():
            for which, src, sem in ((0, kraw, sk), (1, vraw, sv)):
                put(
                    src.at[:, head_cols(h)], kv.at[which, rows_of(own_slot), :],
                    sem, kv_recv.at[own_slot // 2], base + which, spare16.at[which],
                )

    def send_rows(base, h, part):
        @pl.when(part == own_part)
        def _():
            put(kst_src, k_rows.at[own_slot], sks, kst_recv, base, spare32.at[0])

        put(
            st_src.at[h], stats.at[own_pair, :, rows_of(t % 2)],
            ss, st_recv, base + own_core, spare32.at[1],
        )

    def send_queries(base, h, part, sem):
        for which, src in ((1, doraw), (0, qn)):
            put(
                src.at[:, head_cols(h)], qd.at[own_pair, which, rows_of(t % 2), :],
                sem, qd_recv.at[own_pair], base + own_core, spare16.at[2 + which],
            )

    with jax.named_scope("send_kv"):
        for_workers(send_keys)

    with jax.named_scope("wait_z"):
        totals = exchange_z_wait(0)
    with jax.named_scope("send_q"):
        scales = lax.rsqrt(totals / D + EPS)
        kst_src[...] = scales
        for_workers(send_rows)
        scq[...] = row_to_lanes(scales[0:1, :])
        sck[...] = row_to_lanes(scales[1:2, :])
        for h in range(HERE):
            gains[h : h + 1, :] = gain(kg_ref, h)
            qn[:, cols(h)] = (qraw[:, cols(h)].astype(F32) * scq[...] * gain(qg_ref, h)).astype(BF16)


    def turn(j, do):
        for k in range(2):
            x = (cx + j // 2) % 4
            y = across(cy, 2 * (j % 2) + k)
            there, h, part = worker_at(x, y)
            pl.when(there)(functools.partial(do, 2 * (4 * x + y), h, part, sq.at[j, k]))

    def turn_sent(j, _):
        turn(j, lambda base, h, part, sem: wait_for(qd.at[0, 0], sem))
        return 0

    def send_turn(j, _):
        @pl.when(j >= WINDOW)
        def _():
            turn_sent(j - WINDOW, 0)

        turn(j, send_queries)
        return 0

    with jax.named_scope("hold"):
        wait_for(kraw, sk)
        wait_for(vraw, sv)
    with jax.named_scope("send_q0"):
        lax.fori_loop(0, jnp.where(is_worker, LEAD, PAIRS), send_turn, 0)

    @pl.when(is_worker)
    def _():
        with jax.named_scope("wait_kv"):
            acc[...] = jnp.zeros_like(acc)
            r = lax.broadcasted_iota(jnp.int32, (1024, WIN), 0)
            place[...] = (r + WIN * (r // WIN)).astype(F32)

            @pl.when(core == 0)
            def _():
                wait_for(k_rows, kst_recv)

            def forward(c, _):
                piece = kv.at[core, rows_of(c, 256), :]
                wait_for(piece, kv_recv.at[c])

                @pl.when(core == 0)
                def _():
                    for j in range(2):
                        i = 2 * c + j
                        scale = row_to_lanes(k_rows[i, 1:2, :])
                        normed = kv[0, rows_of(i), :].astype(F32) * scale * gains[pl.ds(head, 1), :]
                        kv[0, rows_of(i), :] = normed.astype(BF16)

                pltpu.make_async_remote_copy(
                    src_ref=piece, dst_ref=piece, send_sem=fwd_send, recv_sem=fwd_recv.at[c],
                    device_id={"tm": sibling}, device_id_type=MESH,
                ).start()
                return 0

            lax.fori_loop(0, BLOCKS // 2, forward, 0)

        with jax.named_scope("forward"):

            def forwarded(c, _):
                rows = rows_of(c, 256)
                wait_for(kv.at[1 - core, rows, :], fwd_recv.at[c])
                kt[:, rows] = kv[0, rows, :].T
                return 0

            lax.fori_loop(0, BLOCKS // 2, forwarded, 0)
            wait_for(stats, st_recv)

        def give(c, _):
            sib_out[rows_of(c, 256), :] = acc[1 - core, rows_of(c, 256), :].astype(BF16)
            pltpu.make_async_remote_copy(
                src_ref=sib_out.at[rows_of(c, 256), :], dst_ref=sib_in.at[rows_of(c, 256), :],
                send_sem=sib_send, recv_sem=sib_recv.at[c],
                device_id={"tm": sibling}, device_id_type=MESH,
            ).start()
            return 0

        def finish(c, _):
            rows = rows_of(c, 256)
            pltpu.make_async_copy(sib_in.at[rows, :], sib_in.at[rows, :], sib_recv.at[c]).wait()
            kvout[rows, :] = (acc[core, rows, :] + sib_in[rows, :].astype(F32)).astype(BF16)
            for j in range(2):
                i = 2 * c + j
                put(
                    kvout.at[rows_of(i), :], dkvr.at[core, head],
                    kvs, dkv_recv.at[core], 2 * i + par, spare16.at[5],
                )
            return 0

        def row_of(i):
            return (cx - i // 2 + 4) % 4

        def pair_of(i):
            return 2 * row_of(i) + (cy // 2 + i) % 2

        def done_after(i):
            r = row_of(i)
            ready = ((r > cx) | (cx == 3)).astype(jnp.int32) * (i % 2)
            end = i // (PAIRS - 1)
            lo = ready * (1 - end) * (2 * r + 1 - par)
            hi = ready * jnp.minimum(2 * r + 3 - par, BLOCKS // 2)
            return lo, hi

        def finish_all(lo, hi):
            count = jnp.maximum(hi - lo, 1)
            lax.fori_loop(lo, hi, lambda c, _: finish(lo + (c - lo + 2 * cx) % count, _), 0)

        def pair_step(i, _):
            m = pair_of(i)

            @pl.when(i + LEAD < PAIRS)
            def _():
                send_turn(i + LEAD, 0)

            p = 2 * m + (core + m) % 2
            with jax.named_scope("wait_qd"):
                wait_for(qd.at[m], qd_recv.at[m])
            accq[...] = jnp.zeros_like(accq)

            def work(row, size):
                rows = pl.ds(pl.multiple_of(row, 256), size)
                q = qd[m, 0]
                do = qd[m, 1]
                s = dot(kv[0, rows, :], q, NT)
                probs = jnp.exp2(s * (SCORE_SCALE * LOG2E) - stats[m, 0:1, :])
                limit = stats[m, 2:3, :] - (2 * row + par * WIN).astype(F32)
                at = place[:size, :]
                probs = jnp.where(jnp.concatenate([at, at], axis=1) <= limit, probs, 0.0)
                dp = dot(kv[1, rows, :], do, NT)
                ds = (probs * (dp - stats[m, 1:2, :])).astype(BF16)
                acc[1, rows, :] += dot(probs.astype(BF16), do, NN)
                acc[0, rows, :] += dot(ds, q, NN)
                accq[...] += dot(kt[:, rows], ds, NN)

            blocks = jnp.minimum((p + 3 - par) // 2, BLOCKS // 2)

            def whole(c, _):
                work(c * 1024, 1024)
                return 0

            with jax.named_scope("chunks"):
                lax.fori_loop(0, blocks // 4, whole, 0)

                @pl.when(blocks // 2 % 2 == 1)
                def _():
                    work(blocks // 4 * 1024, 512)

                @pl.when(blocks % 2 == 1)
                def _():
                    work((blocks - 1) * 256, 256)

            dqout[m] = accq[...].T.astype(BF16)

            def back(j, _):
                put(
                    dqout.at[m, rows_of(j), :], dqr.at[par, head],
                    dq_send, dq_recv.at[par], 2 * p + j, spare16.at[4],
                )
                return 0

            lax.fori_loop(0, 2, back, 0)
            lax.fori_loop(*done_after(i), give, 0)

            @pl.when(i > LAG - 1)
            def _():
                finish_all(*done_after(i - LAG))

            return 0

        lax.fori_loop(0, PAIRS, pair_step, 0)
        with jax.named_scope("swap"):
            for i in range(PAIRS - LAG, PAIRS):
                finish_all(*done_after(i))

        with jax.named_scope("worker_waits"):

            wait_for(kv.at[0], fwd_send)
            wait_for(sib_out, sib_send)
            wait_for(kvout, kvs)
            wait_for(dqout, dq_send)

    with jax.named_scope("wait_dq"):
        for i in range(2):
            wait_for(dqr.at[i], dq_recv.at[i])

    part = jnp.zeros((WIN, WIN), F32)
    for h in range(HERE):
        d = (dqr[0, h].astype(F32) + dqr[1, h].astype(F32)) * SCORE_SCALE * gain(qg_ref, h)
        qdn[:, cols(h)] = d
        part = part + qraw[:, cols(h)].astype(F32) * d
    zs[1, 0:1, :] = lanes_to_row(part)
    with jax.named_scope("wait_dk"):
        pltpu.make_async_copy(dkvr.at[0], dkvr.at[0], dkv_recv.at[0]).wait()
    part = jnp.zeros((WIN, WIN), F32)
    for h in range(HERE):
        d = dkvr[0, h].astype(F32) * SCORE_SCALE * gain(kg_ref, h)
        kdn[:, cols(h)] = d
        part = part + kraw[:, cols(h)].astype(F32) * d
    zs[1, 1:2, :] = lanes_to_row(part)
    exchange_z(1)
    with jax.named_scope("wait_dv"):
        pltpu.make_async_copy(dkvr.at[1], dkvr.at[1], dkv_recv.at[1]).wait()
    for h in range(HERE):
        grads_ref[2, :, cols(h)] = dkvr[1, h]
    with jax.named_scope("wait_z2"):
        dots = exchange_z_wait(1) / D
    with jax.named_scope("final"):
        cq = row_to_lanes(dots[0:1, :])
        ck = row_to_lanes(dots[1:2, :])
        for sc, cc, raw, dn, out in (
            (scq, cq, qraw, qdn, 0), (sck, ck, kraw, kdn, 1),
        ):
            s = sc[...]
            coef = s * s * s * cc
            for h in range(HERE):
                grads_ref[out, :, cols(h)] = (
                    s * dn[:, cols(h)] - raw[:, cols(h)].astype(F32) * coef
                ).astype(BF16)

    with jax.named_scope("ends"):

        for which in range(2):
            wait_for(zx.at[which, pl.ds(0, 7)], z_send.at[which])
        wait_for(st_src, sks)
        lax.fori_loop(PAIRS - WINDOW, PAIRS, turn_sent, 0)
        wait_for(stats.at[pl.ds(0, 6)], ss)


def on_device(q, k, v, fo, do, log_sums, group_index, q_gain, k_gain):
    block = (WIN, HERE * HEAD_DIM)
    any_spec = pl.BlockSpec(memory_space=pl.ANY)
    vmem_spec = pl.BlockSpec(memory_space=pltpu.VMEM)
    dma = pltpu.SemaphoreType.DMA
    grads = pl.pallas_call(
        kernel,
        out_shape=pltpu.VMEM((3, *block), BF16),
        in_specs=[any_spec] * 9,
        out_specs=vmem_spec,
        scratch_shapes=[
            *[pltpu.VMEM(block, BF16)] * 6,
            pltpu.VMEM((WIN, WIN), F32),
            pltpu.VMEM((WIN, WIN), F32),
            pltpu.VMEM((2, KEYS, HEAD_DIM), BF16),
            pltpu.VMEM((8, 2, 2 * WIN, HEAD_DIM), BF16),
            pltpu.VMEM((8, 8, 2 * WIN), F32),
            pltpu.VMEM((HERE, 8, WIN), F32),
            pltpu.VMEM((2, 8, WIN), F32),
            pltpu.VMEM((2, 8, 8, WIN), F32),
            pltpu.VMEM((2, KEYS, HEAD_DIM), F32),
            pltpu.VMEM((HEAD_DIM, 2 * WIN), F32),
            pltpu.VMEM((HEAD_DIM, KEYS), BF16),
            pltpu.VMEM((8, 2 * WIN, HEAD_DIM), BF16),
            pltpu.VMEM((KEYS, HEAD_DIM), BF16),
            pltpu.VMEM((KEYS, HEAD_DIM), BF16),
            pltpu.VMEM((KEYS, HEAD_DIM), BF16),
            pltpu.VMEM((2, HERE, WIN, HEAD_DIM), BF16),
            pltpu.VMEM((2, HERE, WIN, HEAD_DIM), BF16),
            pltpu.VMEM(block, F32),
            pltpu.VMEM(block, F32),
            pltpu.VMEM((1024, WIN), F32),
            pltpu.VMEM((BLOCKS, 8, WIN), F32),
            pltpu.VMEM((8, WIN), F32),
            pltpu.VMEM((8, WIN), F32),
            pltpu.VMEM((6, WIN, HEAD_DIM), BF16),
            pltpu.VMEM((2, 8, WIN), F32),
            pltpu.VMEM((HERE, WIN), F32),
            pltpu.VMEM((WINDOWS, WIN), jnp.int32),
            pltpu.VMEM((HERE * HEAD_DIM,), F32),
            pltpu.VMEM((HERE * HEAD_DIM,), F32),
            dma((9,)), dma((2,)), dma((2,)),
            dma, dma, dma((PAIRS, 2)), dma, dma,
            dma, dma((BLOCKS // 2,)), dma, dma((BLOCKS // 2,)),
            dma((8,)), dma, dma, dma((2,)), dma, dma((BLOCKS // 2,)),
            dma, dma((2,)),
        ],
        compiler_params=pltpu.CompilerParams(
            collective_id=0, has_side_effects=True, vmem_limit_bytes=60 << 20
        ),
        cost_estimate=pl.CostEstimate(
            flops=2 * 10**9, bytes_accessed=2 * 10**6, transcendentals=2 * 10**6
        ),
    )(
        q, k, v, fo, do, log_sums, group_index.reshape(WINDOWS, WIN),
        q_gain, k_gain,
    )
    return grads[0], grads[1], grads[2]


def solution(mesh):
    tok, heads = P("tm", "heads"), P("heads")
    return jax.shard_map(
        on_device,
        mesh=mesh,
        in_specs=(tok, tok, tok, tok, tok, P("heads", "tm"), P(), heads, heads),
        out_specs=(tok, tok, tok),
        check_vma=False,
    )
```

```python
import functools
import math

import jax
import jax.numpy as jnp
from jax import lax
from jax.experimental import pallas as pl
from jax.experimental.pallas import tpu as pltpu
from jax.sharding import PartitionSpec as P

D = 6144
HEAD_DIM = 128
EPS = 1e-06
WIN = 128
HERE = 6
WINDOWS = 32
BLOCKS = WINDOWS // 2
KEYS = BLOCKS * WIN
LEAD = 6
WINDOW = 6
FIRST = 4
LAG = 2
PAIRS = 8
MESH = pl.DeviceIdType.MESH
F32 = jnp.float32
BF16 = jnp.bfloat16
LOG2E = math.log2(math.e)
SCORE_SCALE = 1.0 / math.sqrt(HEAD_DIM)
NT = (((1,), (1,)), ((), ()))
NN = (((1,), (0,)), ((), ()))


def dot(a, b, dims):
    return lax.dot_general(a, b, dims, preferred_element_type=F32)


def worker_at(x, y):
    turn = (y - x + 3) % 4
    middle = turn % 2
    head = middle * (4 + x // 2) + (1 - middle) * x
    part = middle * (1 - x % 2) + (1 - middle) * (1 - turn // 2)
    return turn != 3, head, part


def across(y, k):
    return (y // 2 + k // 2) % 2 * 2 + (y + k) % 2


def lanes_to_row(block):
    return jnp.sum(block.T, axis=0, keepdims=True)


def row_to_lanes(row):
    return jnp.broadcast_to(row, (WIN, WIN)).T


def kernel(
    q_hbm, k_hbm, v_hbm, fo_hbm, do_hbm, ls_hbm, grp_hbm, qg_hbm, kg_hbm,
    grads_ref,
    qraw, kraw, vraw, foraw, doraw, qn, scq, sck,
    kv, qd, stats, st_src, zs, zx, acc, accq, kt, dqout, sib_out, sib_in, kvout,
    dqr, dkvr, qdn, kdn,
    place, k_rows, kst_src, gains, spare16, spare32, ls_ref, grp_ref, qg_ref, kg_ref,
    load_sem, z_send, z_recv, sk, sv, sq, ss, sks, kst_recv, kv_recv, fwd_send, fwd_recv,
    qd_recv, st_recv, dq_send, dq_recv, keys_left, sib_send, sib_recv, kvs, dkv_recv,
):
    t = lax.axis_index("tm")
    z = lax.axis_index("heads")
    chip = t // 2
    core = t % 2
    sibling = t + 1 - 2 * core
    cx = chip // 4
    cy = chip % 4
    is_worker, head, par = worker_at(cx, cy)

    loads = [
        pltpu.make_async_copy(src, dst, load_sem.at[i])
        for i, (src, dst) in enumerate(
            (
                (q_hbm, qraw), (k_hbm, kraw), (do_hbm, doraw), (fo_hbm, foraw), (v_hbm, vraw),
                (ls_hbm, ls_ref), (grp_hbm, grp_ref), (qg_hbm, qg_ref), (kg_hbm, kg_ref),
            )
        )
    ]
    for c in loads:
        c.start()
    barrier = pltpu.get_barrier_semaphore()

    def greet_tm(i, _):
        pl.semaphore_signal(barrier, inc=1, device_id={"tm": (t + i) % WINDOWS}, device_id_type=MESH)
        return 0

    def greet_z(i, _):
        pl.semaphore_signal(barrier, inc=1, device_id={"heads": (z + i) % 8}, device_id_type=MESH)
        return 0

    with jax.named_scope("greet"):
        lax.fori_loop(1, 8, greet_z, 0)
        lax.fori_loop(1, WINDOWS, greet_tm, 0)

    def cols(h):
        return slice(h * HEAD_DIM, (h + 1) * HEAD_DIM)

    def gain(ref, h):
        return ref[pl.ds(h * HEAD_DIM, HEAD_DIM)].reshape(1, HEAD_DIM)

    with jax.named_scope("sums"):
        loads[0].wait()
        loads[1].wait()
        zs[...] = jnp.zeros_like(zs)
        for row, raw in ((0, qraw), (1, kraw)):
            total = jnp.zeros((WIN, WIN), F32)
            for h in range(HERE):
                x = raw[:, cols(h)].astype(F32)
                total = total + x * x
            zs[0, row : row + 1, :] = lanes_to_row(total)

    with jax.named_scope("rowdata"):
        loads[2].wait()
        loads[3].wait()
        loads[5].wait()
        loads[6].wait()
        own = grp_ref[pl.ds(t, 1), :].astype(F32)
        nxt = grp_ref[pl.ds(jnp.minimum(t + 1, WINDOWS - 1), 1), :].astype(F32)
        seen = (row_to_lanes(own) <= own).astype(F32)
        seen_next = jnp.where(
            (t < WINDOWS - 1) & (row_to_lanes(nxt) <= own), 1.0, 0.0
        )
        last = (t * WIN - 1).astype(F32) + jnp.sum(seen + seen_next, axis=0, keepdims=True)
        st_src[...] = jnp.zeros_like(st_src)
        for h in range(HERE):
            prod = doraw[:, cols(h)].astype(F32) * foraw[:, cols(h)].astype(F32)
            st_src[h, 0:1, :] = ls_ref[h : h + 1, :] * LOG2E
            st_src[h, 1:2, :] = lanes_to_row(prod)
            st_src[h, 2:3, :] = last
        loads[4].wait()
        loads[7].wait()
        loads[8].wait()

    with jax.named_scope("meet"):
        pl.semaphore_wait(barrier, WINDOWS - 1 + 7)

    def exchange_z(which):
        def send(i, _):
            pltpu.make_async_remote_copy(
                src_ref=zs.at[which], dst_ref=zx.at[which, z],
                send_sem=z_send.at[which], recv_sem=z_recv.at[which],
                device_id={"heads": (z + 1 + (i + 3) % 7) % 8}, device_id_type=MESH,
            ).start()
            return 0

        lax.fori_loop(0, 7, send, 0)
        zx[which, pl.ds(z, 1)] = zs[pl.ds(which, 1)]

    def exchange_z_wait(which):
        part = zx.at[which, pl.ds(0, 7)]
        pltpu.make_async_copy(part, part, z_recv.at[which]).wait()
        return jnp.sum(zx[which], axis=0)

    exchange_z(0)

    def put(src, dst, send_sem, recv_sem, target, spare):
        @pl.when(target == t)
        def _():
            pltpu.make_async_copy(src, dst, recv_sem).start()
            pltpu.make_async_copy(src, spare, send_sem).start()

        @pl.when(target != t)
        def _():
            pltpu.make_async_remote_copy(
                src_ref=src, dst_ref=dst, send_sem=send_sem, recv_sem=recv_sem,
                device_id={"tm": target}, device_id_type=MESH,
            ).start()

    def wait_for(ref, sem):
        pltpu.make_async_copy(ref, ref, sem).wait()

    def rows_of(i, size=WIN):
        return pl.ds(pl.multiple_of(i * size, size), size)

    def head_cols(h):
        return pl.ds(pl.multiple_of(h * HEAD_DIM, HEAD_DIM), HEAD_DIM)

    own_part = t % 2
    own_slot = t // 2
    own_pair = t // 4
    own_core = (t // 2 + t // 4) % 2

    def for_workers(do):
        def step(i, _):
            x = (cx + i // 4) % 4
            y = (cy + i % 4) % 4
            there, h, part = worker_at(x, y)
            pl.when(there)(functools.partial(do, 2 * (4 * x + y), h, part))
            return 0

        lax.fori_loop(0, 16, step, 0)

    def send_keys(base, h, part):
        @pl.when(part == own_part)
        def _():
            for which, src, sem in ((0, kraw, sk), (1, vraw, sv)):
                put(
                    src.at[:, head_cols(h)], kv.at[which, rows_of(own_slot), :],
                    sem, kv_recv.at[own_slot // 2], base + which, spare16.at[which],
                )

    def send_rows(base, h, part):
        @pl.when(part == own_part)
        def _():
            put(kst_src, k_rows.at[own_slot], sks, kst_recv, base, spare32.at[0])

        put(
            st_src.at[h], stats.at[own_pair, :, rows_of(t % 2)],
            ss, st_recv, base + own_core, spare32.at[1],
        )

    def send_queries(base, h, part, sem):
        for which, src in ((1, doraw), (0, qn)):
            put(
                src.at[:, head_cols(h)], qd.at[own_pair, which, rows_of(t % 2), :],
                sem, qd_recv.at[own_pair], base + own_core, spare16.at[2 + which],
            )

    with jax.named_scope("send_kv"):
        for_workers(send_keys)

    with jax.named_scope("wait_z"):
        totals = exchange_z_wait(0)
    with jax.named_scope("send_q"):
        scales = lax.rsqrt(totals / D + EPS)
        kst_src[...] = scales
        for_workers(send_rows)
        scq[...] = row_to_lanes(scales[0:1, :])
        sck[...] = row_to_lanes(scales[1:2, :])
        for h in range(HERE):
            gains[h : h + 1, :] = gain(kg_ref, h)
            qn[:, cols(h)] = (qraw[:, cols(h)].astype(F32) * scq[...] * gain(qg_ref, h)).astype(BF16)


    def turn(j, do):
        for k in range(2):
            x = (cx + j // 2) % 4
            y = across(cy, 2 * (j % 2) + k)
            there, h, part = worker_at(x, y)
            pl.when(there)(functools.partial(do, 2 * (4 * x + y), h, part, sq.at[j, k]))

    def turn_sent(j, _):
        turn(j, lambda base, h, part, sem: wait_for(qd.at[0, 0], sem))
        return 0

    def send_turn(j, _):
        @pl.when(j >= WINDOW)
        def _():
            turn_sent(j - WINDOW, 0)

        turn(j, send_queries)
        return 0

    with jax.named_scope("hold"):
        wait_for(kraw, sk)
        wait_for(vraw, sv)
    with jax.named_scope("send_q0"):
        lax.fori_loop(0, jnp.where(is_worker, FIRST, PAIRS), send_turn, 0)

    @pl.when(is_worker)
    def _():
        with jax.named_scope("wait_kv"):
            acc[...] = jnp.zeros_like(acc)
            r = lax.broadcasted_iota(jnp.int32, (1024, WIN), 0)
            place[...] = (r + WIN * (r // WIN)).astype(F32)

            @pl.when(core == 0)
            def _():
                wait_for(k_rows, kst_recv)

            def forward(c, _):
                piece = kv.at[core, rows_of(c, 256), :]
                wait_for(piece, kv_recv.at[c])

                @pl.when(core == 0)
                def _():
                    for j in range(2):
                        i = 2 * c + j
                        scale = row_to_lanes(k_rows[i, 1:2, :])
                        normed = kv[0, rows_of(i), :].astype(F32) * scale * gains[pl.ds(head, 1), :]
                        kv[0, rows_of(i), :] = normed.astype(BF16)

                pltpu.make_async_remote_copy(
                    src_ref=piece, dst_ref=piece, send_sem=fwd_send, recv_sem=fwd_recv.at[c],
                    device_id={"tm": sibling}, device_id_type=MESH,
                ).start()
                return 0

            lax.fori_loop(0, BLOCKS // 2, forward, 0)

        lax.fori_loop(FIRST, LEAD, send_turn, 0)
        with jax.named_scope("forward"):

            def forwarded(c, _):
                rows = rows_of(c, 256)
                wait_for(kv.at[1 - core, rows, :], fwd_recv.at[c])
                kt[:, rows] = kv[0, rows, :].T
                return 0

            lax.fori_loop(0, BLOCKS // 2, forwarded, 0)
            wait_for(stats, st_recv)

        def give(c, _):
            sib_out[rows_of(c, 256), :] = acc[1 - core, rows_of(c, 256), :].astype(BF16)
            pltpu.make_async_remote_copy(
                src_ref=sib_out.at[rows_of(c, 256), :], dst_ref=sib_in.at[rows_of(c, 256), :],
                send_sem=sib_send, recv_sem=sib_recv.at[c],
                device_id={"tm": sibling}, device_id_type=MESH,
            ).start()
            return 0

        def finish(c, _):
            rows = rows_of(c, 256)
            pltpu.make_async_copy(sib_in.at[rows, :], sib_in.at[rows, :], sib_recv.at[c]).wait()
            kvout[rows, :] = (acc[core, rows, :] + sib_in[rows, :].astype(F32)).astype(BF16)
            for j in range(2):
                i = 2 * c + j
                put(
                    kvout.at[rows_of(i), :], dkvr.at[core, head],
                    kvs, dkv_recv.at[core], 2 * i + par, spare16.at[5],
                )
            return 0

        def row_of(i):
            return (cx - i // 2 + 4) % 4

        def pair_of(i):
            return 2 * row_of(i) + (cy // 2 + i) % 2

        def done_after(i):
            r = row_of(i)
            ready = ((r > cx) | (cx == 3)).astype(jnp.int32) * (i % 2)
            end = i // (PAIRS - 1)
            lo = ready * (1 - end) * (2 * r + 1 - par)
            hi = ready * jnp.minimum(2 * r + 3 - par, BLOCKS // 2)
            return lo, hi

        def finish_all(lo, hi):
            count = jnp.maximum(hi - lo, 1)
            lax.fori_loop(lo, hi, lambda c, _: finish(lo + (c - lo + 2 * cx) % count, _), 0)

        def pair_step(i, _):
            m = pair_of(i)

            @pl.when(i + LEAD < PAIRS)
            def _():
                send_turn(i + LEAD, 0)

            p = 2 * m + (core + m) % 2
            with jax.named_scope("wait_qd"):
                wait_for(qd.at[m], qd_recv.at[m])
            accq[...] = jnp.zeros_like(accq)

            def work(row, size):
                rows = pl.ds(pl.multiple_of(row, 256), size)
                q = qd[m, 0]
                do = qd[m, 1]
                s = dot(kv[0, rows, :], q, NT)
                probs = jnp.exp2(s * (SCORE_SCALE * LOG2E) - stats[m, 0:1, :])
                limit = stats[m, 2:3, :] - (2 * row + par * WIN).astype(F32)
                at = place[:size, :]
                probs = jnp.where(jnp.concatenate([at, at], axis=1) <= limit, probs, 0.0)
                dp = dot(kv[1, rows, :], do, NT)
                ds = (probs * (dp - stats[m, 1:2, :])).astype(BF16)
                acc[1, rows, :] += dot(probs.astype(BF16), do, NN)
                acc[0, rows, :] += dot(ds, q, NN)
                accq[...] += dot(kt[:, rows], ds, NN)

            blocks = jnp.minimum((p + 3 - par) // 2, BLOCKS // 2)

            def whole(c, _):
                work(c * 1024, 1024)
                return 0

            with jax.named_scope("chunks"):
                lax.fori_loop(0, blocks // 4, whole, 0)

                @pl.when(blocks // 2 % 2 == 1)
                def _():
                    work(blocks // 4 * 1024, 512)

                @pl.when(blocks % 2 == 1)
                def _():
                    work((blocks - 1) * 256, 256)

            dqout[m] = accq[...].T.astype(BF16)

            def back(j, _):
                put(
                    dqout.at[m, rows_of(j), :], dqr.at[par, head],
                    dq_send, dq_recv.at[par], 2 * p + j, spare16.at[4],
                )
                return 0

            lax.fori_loop(0, 2, back, 0)
            lax.fori_loop(*done_after(i), give, 0)

            @pl.when(i > LAG - 1)
            def _():
                finish_all(*done_after(i - LAG))

            return 0

        lax.fori_loop(0, PAIRS, pair_step, 0)
        with jax.named_scope("swap"):
            finish_all(*done_after(PAIRS - 2))

            @pl.when(core == 1)
            def _():
                pl.semaphore_wait(keys_left, 1)

            finish_all(*done_after(PAIRS - 1))

            @pl.when(core == 0)
            def _():
                wait_for(kvout, kvs)
                pl.semaphore_signal(
                    keys_left, inc=1, device_id={"tm": sibling}, device_id_type=MESH
                )

    with jax.named_scope("wait_dq"):
        for i in range(2):
            wait_for(dqr.at[i], dq_recv.at[i])

    part = jnp.zeros((WIN, WIN), F32)
    for h in range(HERE):
        d = (dqr[0, h].astype(F32) + dqr[1, h].astype(F32)) * SCORE_SCALE * gain(qg_ref, h)
        qdn[:, cols(h)] = d
        part = part + qraw[:, cols(h)].astype(F32) * d
    zs[1, 0:1, :] = lanes_to_row(part)
    with jax.named_scope("wait_dk"):
        pltpu.make_async_copy(dkvr.at[0], dkvr.at[0], dkv_recv.at[0]).wait()
    part = jnp.zeros((WIN, WIN), F32)
    for h in range(HERE):
        d = dkvr[0, h].astype(F32) * SCORE_SCALE * gain(kg_ref, h)
        kdn[:, cols(h)] = d
        part = part + kraw[:, cols(h)].astype(F32) * d
    zs[1, 1:2, :] = lanes_to_row(part)
    exchange_z(1)
    with jax.named_scope("wait_dv"):
        pltpu.make_async_copy(dkvr.at[1], dkvr.at[1], dkv_recv.at[1]).wait()
    for h in range(HERE):
        grads_ref[2, :, cols(h)] = dkvr[1, h]
    with jax.named_scope("wait_z2"):
        dots = exchange_z_wait(1) / D
    with jax.named_scope("final"):
        cq = row_to_lanes(dots[0:1, :])
        ck = row_to_lanes(dots[1:2, :])
        for sc, cc, raw, dn, out in (
            (scq, cq, qraw, qdn, 0), (sck, ck, kraw, kdn, 1),
        ):
            s = sc[...]
            coef = s * s * s * cc
            for h in range(HERE):
                grads_ref[out, :, cols(h)] = (
                    s * dn[:, cols(h)] - raw[:, cols(h)].astype(F32) * coef
                ).astype(BF16)

    with jax.named_scope("ends"):

        @pl.when(is_worker)
        def _():
            wait_for(kv.at[0], fwd_send)
            wait_for(sib_out, sib_send)
            pl.when(core == 1)(functools.partial(wait_for, kvout, kvs))
            wait_for(dqout, dq_send)


        for which in range(2):
            wait_for(zx.at[which, pl.ds(0, 7)], z_send.at[which])
        wait_for(st_src, sks)
        lax.fori_loop(PAIRS - WINDOW, PAIRS, turn_sent, 0)
        wait_for(stats.at[pl.ds(0, 6)], ss)


def on_device(q, k, v, fo, do, log_sums, group_index, q_gain, k_gain):
    block = (WIN, HERE * HEAD_DIM)
    any_spec = pl.BlockSpec(memory_space=pl.ANY)
    vmem_spec = pl.BlockSpec(memory_space=pltpu.VMEM)
    dma = pltpu.SemaphoreType.DMA
    grads = pl.pallas_call(
        kernel,
        out_shape=pltpu.VMEM((3, *block), BF16),
        in_specs=[any_spec] * 9,
        out_specs=vmem_spec,
        scratch_shapes=[
            *[pltpu.VMEM(block, BF16)] * 6,
            pltpu.VMEM((WIN, WIN), F32),
            pltpu.VMEM((WIN, WIN), F32),
            pltpu.VMEM((2, KEYS, HEAD_DIM), BF16),
            pltpu.VMEM((8, 2, 2 * WIN, HEAD_DIM), BF16),
            pltpu.VMEM((8, 8, 2 * WIN), F32),
            pltpu.VMEM((HERE, 8, WIN), F32),
            pltpu.VMEM((2, 8, WIN), F32),
            pltpu.VMEM((2, 8, 8, WIN), F32),
            pltpu.VMEM((2, KEYS, HEAD_DIM), F32),
            pltpu.VMEM((HEAD_DIM, 2 * WIN), F32),
            pltpu.VMEM((HEAD_DIM, KEYS), BF16),
            pltpu.VMEM((8, 2 * WIN, HEAD_DIM), BF16),
            pltpu.VMEM((KEYS, HEAD_DIM), BF16),
            pltpu.VMEM((KEYS, HEAD_DIM), BF16),
            pltpu.VMEM((KEYS, HEAD_DIM), BF16),
            pltpu.VMEM((2, HERE, WIN, HEAD_DIM), BF16),
            pltpu.VMEM((2, HERE, WIN, HEAD_DIM), BF16),
            pltpu.VMEM(block, F32),
            pltpu.VMEM(block, F32),
            pltpu.VMEM((1024, WIN), F32),
            pltpu.VMEM((BLOCKS, 8, WIN), F32),
            pltpu.VMEM((8, WIN), F32),
            pltpu.VMEM((8, WIN), F32),
            pltpu.VMEM((6, WIN, HEAD_DIM), BF16),
            pltpu.VMEM((2, 8, WIN), F32),
            pltpu.VMEM((HERE, WIN), F32),
            pltpu.VMEM((WINDOWS, WIN), jnp.int32),
            pltpu.VMEM((HERE * HEAD_DIM,), F32),
            pltpu.VMEM((HERE * HEAD_DIM,), F32),
            dma((9,)), dma((2,)), dma((2,)),
            dma, dma, dma((PAIRS, 2)), dma, dma,
            dma, dma((BLOCKS // 2,)), dma, dma((BLOCKS // 2,)),
            dma((8,)), dma, dma, dma((2,)), pltpu.SemaphoreType.REGULAR, dma, dma((BLOCKS // 2,)),
            dma, dma((2,)),
        ],
        compiler_params=pltpu.CompilerParams(
            collective_id=0, has_side_effects=True, vmem_limit_bytes=60 << 20
        ),
        cost_estimate=pl.CostEstimate(
            flops=2 * 10**9, bytes_accessed=2 * 10**6, transcendentals=2 * 10**6
        ),
    )(
        q, k, v, fo, do, log_sums, group_index.reshape(WINDOWS, WIN),
        q_gain, k_gain,
    )
    return grads[0], grads[1], grads[2]


def solution(mesh):
    tok, heads = P("tm", "heads"), P("heads")
    return jax.shard_map(
        on_device,
        mesh=mesh,
        in_specs=(tok, tok, tok, tok, tok, P("heads", "tm"), P(), heads, heads),
        out_specs=(tok, tok, tok),
        check_vma=False,
    )
```

```python
import functools
import math

import jax
import jax.numpy as jnp
from jax import lax
from jax.experimental import pallas as pl
from jax.experimental.pallas import tpu as pltpu
from jax.sharding import PartitionSpec as P

D = 6144
HEAD_DIM = 128
EPS = 1e-06
WIN = 128
HERE = 6
WINDOWS = 32
BLOCKS = WINDOWS // 2
KEYS = BLOCKS * WIN
LEAD = 5
WINDOW = 6
FIRST = 4
LAG = 2
PAIRS = 8
MESH = pl.DeviceIdType.MESH
F32 = jnp.float32
BF16 = jnp.bfloat16
LOG2E = math.log2(math.e)
SCORE_SCALE = 1.0 / math.sqrt(HEAD_DIM)
NT = (((1,), (1,)), ((), ()))
NN = (((1,), (0,)), ((), ()))


def dot(a, b, dims):
    return lax.dot_general(a, b, dims, preferred_element_type=F32)


def worker_at(x, y):
    turn = (y - x + 3) % 4
    middle = turn % 2
    head = middle * (4 + x // 2) + (1 - middle) * x
    part = middle * (1 - x % 2) + (1 - middle) * (1 - turn // 2)
    return turn != 3, head, part


def across(y, k):
    return (y // 2 + k // 2) % 2 * 2 + (y + k) % 2


def lanes_to_row(block):
    return jnp.sum(block.T, axis=0, keepdims=True)


def row_to_lanes(row):
    return jnp.broadcast_to(row, (WIN, WIN)).T


def kernel(
    q_hbm, k_hbm, v_hbm, fo_hbm, do_hbm, ls_hbm, grp_hbm, qg_hbm, kg_hbm,
    grads_ref,
    qraw, kraw, vraw, foraw, doraw, qn, scq, sck,
    kv, qd, stats, st_src, zs, zx, acc, accq, kt, dqout, sib_out, sib_in, kvout,
    dqr, dkvr, qdn, kdn,
    place, k_rows, kst_src, gains, spare16, spare32, ls_ref, grp_ref, qg_ref, kg_ref,
    load_sem, z_send, z_recv, sk, sv, sq, ss, sks, kst_recv, kv_recv, fwd_send, fwd_recv,
    qd_recv, st_recv, dq_send, dq_recv, keys_left, sib_send, sib_recv, kvs, dkv_recv,
):
    t = lax.axis_index("tm")
    z = lax.axis_index("heads")
    chip = t // 2
    core = t % 2
    sibling = t + 1 - 2 * core
    cx = chip // 4
    cy = chip % 4
    is_worker, head, par = worker_at(cx, cy)

    loads = [
        pltpu.make_async_copy(src, dst, load_sem.at[i])
        for i, (src, dst) in enumerate(
            (
                (q_hbm, qraw), (k_hbm, kraw), (do_hbm, doraw), (fo_hbm, foraw), (v_hbm, vraw),
                (ls_hbm, ls_ref), (grp_hbm, grp_ref), (qg_hbm, qg_ref), (kg_hbm, kg_ref),
            )
        )
    ]
    barrier = pltpu.get_barrier_semaphore()

    def greet_tm(i, _):
        other = (t + 1 + (i + 15) % (WINDOWS - 1)) % WINDOWS
        pl.semaphore_signal(barrier, inc=1, device_id={"tm": other}, device_id_type=MESH)
        return 0

    def greet_z(i, _):
        other = (z + 1 + (i + 3) % 7) % 8
        pl.semaphore_signal(barrier, inc=1, device_id={"heads": other}, device_id_type=MESH)
        return 0

    with jax.named_scope("greet"):
        lax.fori_loop(0, 7, greet_z, 0)
        lax.fori_loop(0, WINDOWS - 1, greet_tm, 0)
        for c in loads:
            c.start()

    def cols(h):
        return slice(h * HEAD_DIM, (h + 1) * HEAD_DIM)

    def gain(ref, h):
        return ref[pl.ds(h * HEAD_DIM, HEAD_DIM)].reshape(1, HEAD_DIM)

    with jax.named_scope("sums"):
        loads[0].wait()
        loads[1].wait()
        zs[...] = jnp.zeros_like(zs)
        for row, raw in ((0, qraw), (1, kraw)):
            total = jnp.zeros((WIN, WIN), F32)
            for h in range(HERE):
                x = raw[:, cols(h)].astype(F32)
                total = total + x * x
            zs[0, row : row + 1, :] = lanes_to_row(total)

    with jax.named_scope("rowdata"):
        loads[2].wait()
        loads[3].wait()
        loads[5].wait()
        loads[6].wait()
        own = grp_ref[pl.ds(t, 1), :].astype(F32)
        nxt = grp_ref[pl.ds(jnp.minimum(t + 1, WINDOWS - 1), 1), :].astype(F32)
        seen = (row_to_lanes(own) <= own).astype(F32)
        seen_next = jnp.where(
            (t < WINDOWS - 1) & (row_to_lanes(nxt) <= own), 1.0, 0.0
        )
        last = (t * WIN - 1).astype(F32) + jnp.sum(seen + seen_next, axis=0, keepdims=True)
        st_src[...] = jnp.zeros_like(st_src)
        for h in range(HERE):
            prod = doraw[:, cols(h)].astype(F32) * foraw[:, cols(h)].astype(F32)
            st_src[h, 0:1, :] = ls_ref[h : h + 1, :] * LOG2E
            st_src[h, 1:2, :] = lanes_to_row(prod)
            st_src[h, 2:3, :] = last
        loads[4].wait()
        loads[7].wait()
        loads[8].wait()

    with jax.named_scope("meet"):
        pl.semaphore_wait(barrier, WINDOWS - 1 + 7)

    def exchange_z(which):
        def send(i, _):
            pltpu.make_async_remote_copy(
                src_ref=zs.at[which], dst_ref=zx.at[which, z],
                send_sem=z_send.at[which], recv_sem=z_recv.at[which],
                device_id={"heads": (z + 1 + (i + 3) % 7) % 8}, device_id_type=MESH,
            ).start()
            return 0

        lax.fori_loop(0, 7, send, 0)
        zx[which, pl.ds(z, 1)] = zs[pl.ds(which, 1)]

    def exchange_z_wait(which):
        part = zx.at[which, pl.ds(0, 7)]
        pltpu.make_async_copy(part, part, z_recv.at[which]).wait()
        return jnp.sum(zx[which], axis=0)

    exchange_z(0)

    def put(src, dst, send_sem, recv_sem, target, spare):
        @pl.when(target == t)
        def _():
            pltpu.make_async_copy(src, dst, recv_sem).start()
            pltpu.make_async_copy(src, spare, send_sem).start()

        @pl.when(target != t)
        def _():
            pltpu.make_async_remote_copy(
                src_ref=src, dst_ref=dst, send_sem=send_sem, recv_sem=recv_sem,
                device_id={"tm": target}, device_id_type=MESH,
            ).start()

    def wait_for(ref, sem):
        pltpu.make_async_copy(ref, ref, sem).wait()

    def rows_of(i, size=WIN):
        return pl.ds(pl.multiple_of(i * size, size), size)

    def head_cols(h):
        return pl.ds(pl.multiple_of(h * HEAD_DIM, HEAD_DIM), HEAD_DIM)

    own_part = t % 2
    own_slot = t // 2
    own_pair = t // 4
    own_core = (t // 2 + t // 4) % 2

    def for_workers(do):
        def step(i, _):
            x = (cx + i // 4) % 4
            y = (cy + i % 4) % 4
            there, h, part = worker_at(x, y)
            pl.when(there)(functools.partial(do, 2 * (4 * x + y), h, part))
            return 0

        lax.fori_loop(0, 16, step, 0)

    def send_keys(which, src, sem, base, h, part):
        @pl.when(part == own_part)
        def _():
            put(
                src.at[:, head_cols(h)], kv.at[which, rows_of(own_slot), :],
                sem, kv_recv.at[own_slot // 2], base + which, spare16.at[which],
            )

    def send_rows(base, h, part):
        @pl.when(part == own_part)
        def _():
            put(kst_src, k_rows.at[own_slot], sks, kst_recv, base, spare32.at[0])

        put(
            st_src.at[h], stats.at[own_pair, :, rows_of(t % 2)],
            ss, st_recv, base + own_core, spare32.at[1],
        )

    def send_queries(base, h, part, sem):
        for which, src in ((1, doraw), (0, qn)):
            put(
                src.at[:, head_cols(h)], qd.at[own_pair, which, rows_of(t % 2), :],
                sem, qd_recv.at[own_pair], base + own_core, spare16.at[2 + which],
            )

    with jax.named_scope("send_kv"):
        for_workers(functools.partial(send_keys, 0, kraw, sk))
        for_workers(functools.partial(send_keys, 1, vraw, sv))

    with jax.named_scope("wait_z"):
        totals = exchange_z_wait(0)
    with jax.named_scope("send_q"):
        scales = lax.rsqrt(totals / D + EPS)
        kst_src[...] = scales
        for_workers(send_rows)
        scq[...] = row_to_lanes(scales[0:1, :])
        sck[...] = row_to_lanes(scales[1:2, :])
        for h in range(HERE):
            gains[h : h + 1, :] = gain(kg_ref, h)
            qn[:, cols(h)] = (qraw[:, cols(h)].astype(F32) * scq[...] * gain(qg_ref, h)).astype(BF16)


    def turn(j, do):
        for k in range(2):
            x = (cx + j // 2) % 4
            y = across(cy, 2 * (j % 2) + k)
            there, h, part = worker_at(x, y)
            pl.when(there)(functools.partial(do, 2 * (4 * x + y), h, part, sq.at[j, k]))

    def turn_sent(j, _):
        turn(j, lambda base, h, part, sem: wait_for(qd.at[0, 0], sem))
        return 0

    def send_turn(j, _):
        @pl.when(j >= WINDOW)
        def _():
            turn_sent(j - WINDOW, 0)

        turn(j, send_queries)
        return 0

    with jax.named_scope("hold"):
        wait_for(kraw, sk)
        wait_for(vraw, sv)
    with jax.named_scope("send_q0"):
        lax.fori_loop(0, jnp.where(is_worker, FIRST, PAIRS), send_turn, 0)

    @pl.when(is_worker)
    def _():
        with jax.named_scope("wait_kv"):
            acc[...] = jnp.zeros_like(acc)
            r = lax.broadcasted_iota(jnp.int32, (1024, WIN), 0)
            place[...] = (r + WIN * (r // WIN)).astype(F32)

            @pl.when(core == 0)
            def _():
                wait_for(k_rows, kst_recv)

            def forward(c, _):
                piece = kv.at[core, rows_of(c, 256), :]
                wait_for(piece, kv_recv.at[c])

                @pl.when(core == 0)
                def _():
                    for j in range(2):
                        i = 2 * c + j
                        scale = row_to_lanes(k_rows[i, 1:2, :])
                        normed = kv[0, rows_of(i), :].astype(F32) * scale * gains[pl.ds(head, 1), :]
                        kv[0, rows_of(i), :] = normed.astype(BF16)

                pltpu.make_async_remote_copy(
                    src_ref=piece, dst_ref=piece, send_sem=fwd_send, recv_sem=fwd_recv.at[c],
                    device_id={"tm": sibling}, device_id_type=MESH,
                ).start()
                return 0

            lax.fori_loop(0, BLOCKS // 2, forward, 0)

        lax.fori_loop(FIRST, LEAD, send_turn, 0)
        with jax.named_scope("forward"):

            def forwarded(c, _):
                rows = rows_of(c, 256)
                wait_for(kv.at[1 - core, rows, :], fwd_recv.at[c])
                kt[:, rows] = kv[0, rows, :].T
                return 0

            lax.fori_loop(0, BLOCKS // 2, forwarded, 0)
            wait_for(stats, st_recv)

        def give(c, _):
            sib_out[rows_of(c, 256), :] = acc[1 - core, rows_of(c, 256), :].astype(BF16)
            pltpu.make_async_remote_copy(
                src_ref=sib_out.at[rows_of(c, 256), :], dst_ref=sib_in.at[rows_of(c, 256), :],
                send_sem=sib_send, recv_sem=sib_recv.at[c],
                device_id={"tm": sibling}, device_id_type=MESH,
            ).start()
            return 0

        def finish(c, _):
            rows = rows_of(c, 256)
            pltpu.make_async_copy(sib_in.at[rows, :], sib_in.at[rows, :], sib_recv.at[c]).wait()
            kvout[rows, :] = (acc[core, rows, :] + sib_in[rows, :].astype(F32)).astype(BF16)
            for j in range(2):
                i = 2 * c + j
                put(
                    kvout.at[rows_of(i), :], dkvr.at[core, head],
                    kvs, dkv_recv.at[core], 2 * i + par, spare16.at[5],
                )
            return 0

        def row_of(i):
            return (cx - i // 2 + 4) % 4

        def pair_of(i):
            return 2 * row_of(i) + (cy // 2 + i) % 2

        def done_after(i):
            r = row_of(i)
            ready = ((r > cx) | (cx == 3)).astype(jnp.int32) * (i % 2)
            end = i // (PAIRS - 1)
            lo = ready * (1 - end) * (2 * r + 1 - par)
            hi = ready * jnp.minimum(2 * r + 3 - par, BLOCKS // 2)
            return lo, hi

        def finish_all(lo, hi):
            count = jnp.maximum(hi - lo, 1)
            lax.fori_loop(lo, hi, lambda c, _: finish(lo + (c - lo + 2 * cx) % count, _), 0)

        def pair_step(i, _):
            m = pair_of(i)

            @pl.when(i + LEAD < PAIRS)
            def _():
                send_turn(i + LEAD, 0)

            p = 2 * m + (core + m) % 2
            with jax.named_scope("wait_qd"):
                wait_for(qd.at[m], qd_recv.at[m])
            accq[...] = jnp.zeros_like(accq)

            def work(row, size):
                rows = pl.ds(pl.multiple_of(row, 256), size)
                q = qd[m, 0]
                do = qd[m, 1]
                s = dot(kv[0, rows, :], q, NT)
                probs = jnp.exp2(s * (SCORE_SCALE * LOG2E) - stats[m, 0:1, :])
                limit = stats[m, 2:3, :] - (2 * row + par * WIN).astype(F32)
                at = place[:size, :]
                probs = jnp.where(jnp.concatenate([at, at], axis=1) <= limit, probs, 0.0)
                dp = dot(kv[1, rows, :], do, NT)
                ds = (probs * (dp - stats[m, 1:2, :])).astype(BF16)
                acc[1, rows, :] += dot(probs.astype(BF16), do, NN)
                acc[0, rows, :] += dot(ds, q, NN)
                accq[...] += dot(kt[:, rows], ds, NN)

            blocks = jnp.minimum((p + 3 - par) // 2, BLOCKS // 2)

            def whole(c, _):
                work(c * 1024, 1024)
                return 0

            with jax.named_scope("chunks"):
                lax.fori_loop(0, blocks // 4, whole, 0)

                @pl.when(blocks // 2 % 2 == 1)
                def _():
                    work(blocks // 4 * 1024, 512)

                @pl.when(blocks % 2 == 1)
                def _():
                    work((blocks - 1) * 256, 256)

            dqout[m] = accq[...].T.astype(BF16)

            def back(j, _):
                put(
                    dqout.at[m, rows_of(j), :], dqr.at[par, head],
                    dq_send, dq_recv.at[par], 2 * p + j, spare16.at[4],
                )
                return 0

            lax.fori_loop(0, 2, back, 0)
            lax.fori_loop(*done_after(i), give, 0)

            @pl.when(i > LAG - 1)
            def _():
                finish_all(*done_after(i - LAG))

            return 0

        lax.fori_loop(0, PAIRS, pair_step, 0)
        with jax.named_scope("swap"):
            finish_all(*done_after(PAIRS - 2))

            @pl.when(core == 1)
            def _():
                pl.semaphore_wait(keys_left, 1)

            finish_all(*done_after(PAIRS - 1))

            @pl.when(core == 0)
            def _():
                wait_for(kvout, kvs)
                pl.semaphore_signal(
                    keys_left, inc=1, device_id={"tm": sibling}, device_id_type=MESH
                )

    with jax.named_scope("wait_dq"):
        for i in range(2):
            wait_for(dqr.at[i], dq_recv.at[i])

    part = jnp.zeros((WIN, WIN), F32)
    for h in range(HERE):
        d = (dqr[0, h].astype(F32) + dqr[1, h].astype(F32)) * SCORE_SCALE * gain(qg_ref, h)
        qdn[:, cols(h)] = d
        part = part + qraw[:, cols(h)].astype(F32) * d
    zs[1, 0:1, :] = lanes_to_row(part)
    with jax.named_scope("wait_dk"):
        pltpu.make_async_copy(dkvr.at[0], dkvr.at[0], dkv_recv.at[0]).wait()
    part = jnp.zeros((WIN, WIN), F32)
    for h in range(HERE):
        d = dkvr[0, h].astype(F32) * SCORE_SCALE * gain(kg_ref, h)
        kdn[:, cols(h)] = d
        part = part + kraw[:, cols(h)].astype(F32) * d
    zs[1, 1:2, :] = lanes_to_row(part)
    exchange_z(1)
    with jax.named_scope("wait_dv"):
        pltpu.make_async_copy(dkvr.at[1], dkvr.at[1], dkv_recv.at[1]).wait()
    for h in range(HERE):
        grads_ref[2, :, cols(h)] = dkvr[1, h]
    with jax.named_scope("wait_z2"):
        dots = exchange_z_wait(1) / D
    with jax.named_scope("final"):
        cq = row_to_lanes(dots[0:1, :])
        ck = row_to_lanes(dots[1:2, :])
        for sc, cc, raw, dn, out in (
            (scq, cq, qraw, qdn, 0), (sck, ck, kraw, kdn, 1),
        ):
            s = sc[...]
            coef = s * s * s * cc
            for h in range(HERE):
                grads_ref[out, :, cols(h)] = (
                    s * dn[:, cols(h)] - raw[:, cols(h)].astype(F32) * coef
                ).astype(BF16)

    with jax.named_scope("ends"):

        @pl.when(is_worker)
        def _():
            wait_for(kv.at[0], fwd_send)
            wait_for(sib_out, sib_send)
            pl.when(core == 1)(functools.partial(wait_for, kvout, kvs))
            wait_for(dqout, dq_send)


        for which in range(2):
            wait_for(zx.at[which, pl.ds(0, 7)], z_send.at[which])
        wait_for(st_src, sks)
        lax.fori_loop(PAIRS - WINDOW, PAIRS, turn_sent, 0)
        wait_for(stats.at[pl.ds(0, 6)], ss)


def on_device(q, k, v, fo, do, log_sums, group_index, q_gain, k_gain):
    block = (WIN, HERE * HEAD_DIM)
    any_spec = pl.BlockSpec(memory_space=pl.ANY)
    vmem_spec = pl.BlockSpec(memory_space=pltpu.VMEM)
    dma = pltpu.SemaphoreType.DMA
    grads = pl.pallas_call(
        kernel,
        out_shape=pltpu.VMEM((3, *block), BF16),
        in_specs=[any_spec] * 9,
        out_specs=vmem_spec,
        scratch_shapes=[
            *[pltpu.VMEM(block, BF16)] * 6,
            pltpu.VMEM((WIN, WIN), F32),
            pltpu.VMEM((WIN, WIN), F32),
            pltpu.VMEM((2, KEYS, HEAD_DIM), BF16),
            pltpu.VMEM((8, 2, 2 * WIN, HEAD_DIM), BF16),
            pltpu.VMEM((8, 8, 2 * WIN), F32),
            pltpu.VMEM((HERE, 8, WIN), F32),
            pltpu.VMEM((2, 8, WIN), F32),
            pltpu.VMEM((2, 8, 8, WIN), F32),
            pltpu.VMEM((2, KEYS, HEAD_DIM), F32),
            pltpu.VMEM((HEAD_DIM, 2 * WIN), F32),
            pltpu.VMEM((HEAD_DIM, KEYS), BF16),
            pltpu.VMEM((8, 2 * WIN, HEAD_DIM), BF16),
            pltpu.VMEM((KEYS, HEAD_DIM), BF16),
            pltpu.VMEM((KEYS, HEAD_DIM), BF16),
            pltpu.VMEM((KEYS, HEAD_DIM), BF16),
            pltpu.VMEM((2, HERE, WIN, HEAD_DIM), BF16),
            pltpu.VMEM((2, HERE, WIN, HEAD_DIM), BF16),
            pltpu.VMEM(block, F32),
            pltpu.VMEM(block, F32),
            pltpu.VMEM((1024, WIN), F32),
            pltpu.VMEM((BLOCKS, 8, WIN), F32),
            pltpu.VMEM((8, WIN), F32),
            pltpu.VMEM((8, WIN), F32),
            pltpu.VMEM((6, WIN, HEAD_DIM), BF16),
            pltpu.VMEM((2, 8, WIN), F32),
            pltpu.VMEM((HERE, WIN), F32),
            pltpu.VMEM((WINDOWS, WIN), jnp.int32),
            pltpu.VMEM((HERE * HEAD_DIM,), F32),
            pltpu.VMEM((HERE * HEAD_DIM,), F32),
            dma((9,)), dma((2,)), dma((2,)),
            dma, dma, dma((PAIRS, 2)), dma, dma,
            dma, dma((BLOCKS // 2,)), dma, dma((BLOCKS // 2,)),
            dma((8,)), dma, dma, dma((2,)), pltpu.SemaphoreType.REGULAR, dma, dma((BLOCKS // 2,)),
            dma, dma((2,)),
        ],
        compiler_params=pltpu.CompilerParams(
            collective_id=0, has_side_effects=True, vmem_limit_bytes=60 << 20
        ),
        cost_estimate=pl.CostEstimate(
            flops=2 * 10**9, bytes_accessed=2 * 10**6, transcendentals=2 * 10**6
        ),
    )(
        q, k, v, fo, do, log_sums, group_index.reshape(WINDOWS, WIN),
        q_gain, k_gain,
    )
    return grads[0], grads[1], grads[2]


def solution(mesh):
    tok, heads = P("tm", "heads"), P("heads")
    return jax.shard_map(
        on_device,
        mesh=mesh,
        in_specs=(tok, tok, tok, tok, tok, P("heads", "tm"), P(), heads, heads),
        out_specs=(tok, tok, tok),
        check_vma=False,
    )
```
